32 devices in a mesh: span: 4 (over x, core), seq: 4 (over z), mp: 2 (over y).
Axes of the slice: x: 2, y: 2, z: 4, core: 2. Of those that a mesh axis runs over, the one named last changes fastest.
Arguments:
- queries: bfloat16 [4, 256, 3072], P('span', 'seq', 'mp'), may hold values from -256 to 256
- keys_values: bfloat16 [2, 4, 256, 512], P(None, 'span', 'seq', 'mp'), may hold values from -200 to 200
- clip_tokens: int32 [4], replicated, may hold values from 64 to 256, as said below
- noise_level: int32 [4], replicated, may hold values from 0 to 63
- level_gate: bfloat16 [64, 3072], P(None, 'mp'), may hold values from -3 to 3
- out_gain: bfloat16 [3072], P('mp'), may hold values from 0.099609375 to 1.8984375
Outputs:
- layer_out: bfloat16 [4, 256, 3072], P('span', 'seq', 'mp')
The draws below stay inside these ranges and needn't reach their ends.
Inputs may be any that keep to these rules, and one draw needn't show every extreme that they name: `clip_tokens`: each clip's live slots are its first ones; some clip fills all 256 slots.
All inputs are finite; a program needn't handle non-finite values.
Results may differ from the reference program's by a relative error of at most 0.0065.
Values may be sent and summed in bfloat16 or wider, within the bound.
No kernel may reach another device: no remote copies, remote signals or barrier semaphores. Data moves between devices by JAX's collectives and lax.ppermute only.
A program may use at most 64 MiB of HBM per device.

```python
import math
import jax
import jax.numpy as jnp
from jax import lax

HEADS = 24
KVH = 4
HD = 128
LEVELS = 64
TOK_DEV = 64
CLIPS = 4
SLOTS = 256


def shared_tokens(base_key):
    root = jax.random.fold_in(base_key, 11)
    key_one = jax.random.fold_in(root, 1)
    key_two = jax.random.fold_in(root, 2)
    key_three = jax.random.fold_in(root, 3)
    full_shape = (CLIPS, SLOTS, KVH, HD)
    key_rows = jnp.clip(jax.random.normal(key_one, full_shape, jnp.float32), -4.0, 4.0)
    head_top = 3.0
    head_scale = head_top ** (jnp.arange(KVH, dtype=jnp.float32) / max(KVH - 1, 1))
    row_scale = 0.5 * jnp.exp(jax.random.uniform(key_three, (CLIPS, SLOTS, 1, 1), jnp.float32, 0.0, math.log(10.0)))
    value_rows = jnp.clip(jax.random.normal(key_two, full_shape, jnp.float32), -4.0, 4.0) * head_scale[:, None] * row_scale
    return (key_rows, value_rows)


def draw_keys_values(key, part):
    key_rows, value_rows = shared_tokens(key)
    stacked = jnp.stack([key_rows.reshape(CLIPS, SLOTS, KVH * HD), value_rows.reshape(CLIPS, SLOTS, KVH * HD)])
    return stacked.astype(jnp.bfloat16)


def draw_queries(key, part):
    query_key = jax.random.fold_in(key, 23)
    full_shape = (CLIPS, SLOTS, HEADS, HD)
    query_rows = jnp.clip(2.0 * jax.random.normal(query_key, full_shape, jnp.float32), -12.0, 12.0)
    return query_rows.reshape(CLIPS, SLOTS, HEADS * HD).astype(jnp.bfloat16)


def draw_clip_tokens(key, part):
    root = jax.random.fold_in(key, 37)
    lengths = jax.random.randint(jax.random.fold_in(root, 1), (CLIPS,), SLOTS // 4, SLOTS + 1)
    filled = jax.random.randint(jax.random.fold_in(root, 2), (), 0, CLIPS)
    lengths = jnp.where(jnp.arange(CLIPS) == filled, SLOTS, lengths)
    return lengths.astype(jnp.int32)


def place_ends(array, stream_key, low, top_value):
    spot = [jax.random.randint(jax.random.fold_in(stream_key, axis), (), 0, length) for axis, length in enumerate(array.shape)]
    main_axis = array.shape.index(max(array.shape))
    next_to = spot[:main_axis] + [(spot[main_axis] + 1) % array.shape[main_axis]] + spot[main_axis + 1:]
    return array.at[tuple(spot)].set(low).at[tuple(next_to)].set(top_value)


def levels(stream_key, extent, pieces, smallest, largest):
    def one(position, shards_of):
        heights = jax.random.uniform(jax.random.fold_in(jax.random.fold_in(stream_key, 6), position), (shards_of,), jnp.float32, smallest / len(pieces), largest / len(pieces))
        return jnp.repeat(jnp.exp(heights), extent[position] // shards_of).reshape((-1,) + (1,) * (len(extent) - position - 1))

    factor_of = one(*pieces[0])
    for cut in pieces[1:]:
        factor_of = factor_of * one(*cut)
    return factor_of


def centred(stream_key, shape, spread, limit, split=(), kind=jnp.bfloat16):
    gain = levels(stream_key, shape, split, -0.22, 0.18) if split else 1.0
    drawn = jax.random.normal(stream_key, shape, jnp.float32) * spread * gain
    return jnp.minimum(jnp.maximum(drawn, -limit), limit).astype(kind)


def setup_inputs(seed: int = 0) -> dict:
    seeds = jax.random.split(jax.random.key(seed), 7)
    queries = draw_queries(jax.random.fold_in(seeds[6], 71), 0)
    keys_values = draw_keys_values(jax.random.fold_in(seeds[6], 71), 0)
    clip_tokens = draw_clip_tokens(jax.random.fold_in(seeds[6], 71), 0)
    noise_level = place_ends(jax.random.randint(seeds[3], (CLIPS,), 0, LEVELS), jax.random.fold_in(seeds[3], 1), 0, LEVELS - 1).astype(jnp.int32)
    level_gate = centred(seeds[4], (LEVELS, HEADS * HD), 0.5, 3.0, ((1, 2),))
    out_gain = jnp.clip(1.0 + 0.18 * jax.random.normal(seeds[5], (HEADS * HD,), jnp.float32), 0.099609375, 1.8984375).astype(jnp.bfloat16)
    return {"queries": queries, "keys_values": keys_values, "clip_tokens": clip_tokens, "noise_level": noise_level, "level_gate": level_gate, "out_gain": out_gain}


def reference(queries, keys_values, clip_tokens, noise_level, level_gate, out_gain):
    clip_count, slot_count, width = queries.shape
    group_size = HEADS // KVH
    score_scale = 1.0 / math.sqrt(HD)
    key_rows = keys_values[0].astype(jnp.float32).reshape(clip_count * slot_count, KVH, HD)
    value_rows = keys_values[1].astype(jnp.float32).reshape(clip_count * slot_count, KVH, HD)
    positions = jnp.arange(clip_count * slot_count, dtype=jnp.int32)
    holder = positions // slot_count
    slot_index = positions - holder * slot_count
    key_usable = slot_index < clip_tokens[holder]
    block_count = clip_count * slot_count // TOK_DEV
    blocks = queries.reshape(block_count, TOK_DEV, KVH, group_size, HD)

    def one_block(block_index):
        query_rows = lax.dynamic_index_in_dim(blocks, block_index, 0, keepdims=False).astype(jnp.float32)
        own_clip = block_index * TOK_DEV // slot_count
        allowed = key_usable & (holder <= own_clip)
        scores = jnp.einsum('tgrd,kgd->tgrk', query_rows, key_rows) * score_scale
        scores = jnp.where(allowed, scores, -jnp.inf)
        row_max = lax.optimization_barrier(jnp.max(scores, axis=-1, keepdims=True))
        weights = jnp.exp(scores - row_max)
        weight_sum = lax.optimization_barrier(jnp.sum(weights, axis=-1))
        rounded = lax.optimization_barrier(weights.astype(jnp.bfloat16)).astype(jnp.float32)
        mixed = jnp.einsum('tgrk,kgd->tgrd', rounded, value_rows)
        return (mixed / weight_sum[..., None]).reshape(TOK_DEV, width)
    attended = lax.map(one_block, jnp.arange(block_count, dtype=jnp.int32)).reshape(clip_count, slot_count, width)
    mean_square = lax.optimization_barrier(jnp.mean(attended * attended, axis=-1, keepdims=True))
    gate_rows = level_gate[noise_level].astype(jnp.float32)
    normed = attended * lax.rsqrt(mean_square + 1e-06) * out_gain.astype(jnp.float32) * (1.0 + gate_rows[:, None, :])
    usable = jnp.arange(slot_count, dtype=jnp.int32)[None, :] < clip_tokens[:, None]
    return jnp.where(usable[..., None], normed, 0.0).astype(jnp.bfloat16)
```

```python
import functools
import math

import jax
import jax.numpy as jnp
from jax import lax
from jax.experimental import pallas as pl
from jax.experimental.pallas import tpu as pltpu
from jax.sharding import PartitionSpec as P

HD = 128
MASKED = -1e30


def exchanged(shard, axis, by):
    peers = lax.axis_size(axis)
    return lax.ppermute(shard, axis, [(i, i ^ by) for i in range(peers)])


def in_vmem(count):
    return [pl.BlockSpec(memory_space=pltpu.VMEM)] * count


def gate_factor(level, gate_ref, gain_ref):
    levels = gate_ref.shape[0]
    one_hot = (lax.broadcasted_iota(jnp.int32, (16, levels), 1) == level).astype(jnp.bfloat16)
    row = jnp.dot(one_hot, gate_ref[...], preferred_element_type=jnp.float32)[:8]
    return gain_ref[...].astype(jnp.float32) * (1.0 + row)


def attend_kernel(group_size, offsets, tokens_ref, level_ref, q_ref, gate_ref, gain_ref, *refs):
    kv_refs = refs[: len(offsets)]
    attended_ref, squares_ref, factor_ref = refs[len(offsets) :]
    own_clip = lax.axis_index("span")
    own_seq = lax.axis_index("seq")
    rows = q_ref.shape[0]
    piece_keys = kv_refs[0].shape[1]
    kv_heads = kv_refs[0].shape[2] // HD
    to_exponent = math.log2(math.e) / math.sqrt(HD)
    factor_ref[...] = gate_factor(level_ref[own_clip], gate_ref, gain_ref)
    lane = lax.broadcasted_iota(jnp.int32, (1, piece_keys), 1)
    biases = []
    for clip_by, seq_by in offsets:
        clip = own_clip ^ clip_by
        live = tokens_ref[clip] - (own_seq ^ seq_by) * piece_keys
        biases.append(jnp.where(lane < jnp.where(clip <= own_clip, live, 0), 0.0, MASKED))
    bias = jnp.concatenate(biases, axis=1)
    squares = jnp.zeros((rows, HD), jnp.float32)
    for g in range(kv_heads):
        first = g * group_size
        heads = [q_ref[:, (first + r) * HD : (first + r + 1) * HD] for r in range(group_size)]
        query_rows = jnp.concatenate(heads, axis=0)
        lanes = slice(g * HD, (g + 1) * HD)
        key_rows = jnp.concatenate([ref[0, :, lanes] for ref in kv_refs], axis=0)
        value_rows = jnp.concatenate([ref[1, :, lanes] for ref in kv_refs], axis=0)
        scores = lax.dot_general(
            query_rows, key_rows, (((1,), (1,)), ((), ())), preferred_element_type=jnp.float32
        )
        scores = scores + bias
        row_max = jnp.max(scores, axis=1, keepdims=True)
        weights = jnp.exp2((scores - row_max) * to_exponent)
        weight_sum = jnp.sum(weights, axis=1, keepdims=True)
        mixed = jnp.dot(
            weights.astype(jnp.bfloat16), value_rows, preferred_element_type=jnp.float32
        )
        mixed = mixed / weight_sum
        for r in range(group_size):
            block = mixed[r * rows : (r + 1) * rows]
            attended_ref[:, (first + r) * HD : (first + r + 1) * HD] = block
            squares = squares + block * block
    squares_ref[...] = jnp.sum(squares.T, axis=0, keepdims=True)


def finish_kernel(features, tokens_ref, attended_ref, own_ref, other_ref, factor_ref, out_ref):
    own_clip = lax.axis_index("span")
    own_seq = lax.axis_index("seq")
    rows = attended_ref.shape[0]
    mean_square = (own_ref[...] + other_ref[...]) / features
    scale = jnp.broadcast_to(lax.rsqrt(mean_square + 1e-06), (HD, rows)).T
    slot = own_seq * rows + lax.broadcasted_iota(jnp.int32, (rows, HD), 0)
    live = slot < tokens_ref[own_clip]
    for h in range(attended_ref.shape[1] // HD):
        lanes = slice(h * HD, (h + 1) * HD)
        block = attended_ref[:, lanes] * scale * factor_ref[0:1, lanes]
        out_ref[0, :, lanes] = jnp.where(live, block, 0.0).astype(out_ref.dtype)


def by_exchange(queries, keys_values, clip_tokens, noise_level, level_gate, out_gain):
    tokens_here, width = queries.shape[1:]
    kv_heads_here = keys_values.shape[-1] // HD
    group_size = width // HD // kv_heads_here
    own = keys_values[:, 0]
    pieces = {(0, 0): own}
    for seq_by in range(1, lax.axis_size("seq")):
        pieces[0, seq_by] = exchanged(own, "seq", seq_by)
    clip_by = 1
    steps = []
    while clip_by < lax.axis_size("span"):
        steps.append(clip_by)
        clip_by *= 2
    for by in reversed(steps):
        for at in list(pieces):
            pieces[at[0] ^ by, at[1]] = exchanged(pieces[at], "span", by)
    offsets = list(pieces)
    smem = pl.BlockSpec(memory_space=pltpu.SMEM)
    attended, squares, factor = pl.pallas_call(
        functools.partial(attend_kernel, group_size, offsets),
        out_shape=(
            jax.ShapeDtypeStruct((tokens_here, width), jnp.float32),
            jax.ShapeDtypeStruct((1, tokens_here), jnp.float32),
            jax.ShapeDtypeStruct((8, width), jnp.float32),
        ),
        in_specs=[smem, smem] + in_vmem(3 + len(offsets)),
        out_specs=tuple(in_vmem(3)),
        compiler_params=pltpu.CompilerParams(vmem_limit_bytes=40 * 1024 * 1024),
        name="attend",
    )(
        clip_tokens,
        noise_level,
        queries[0],
        level_gate,
        out_gain.reshape(1, width),
        *pieces.values(),
    )
    others = [exchanged(squares, "mp", by) for by in range(1, lax.axis_size("mp"))]
    return pl.pallas_call(
        functools.partial(finish_kernel, width * lax.axis_size("mp")),
        out_shape=jax.ShapeDtypeStruct(queries.shape, queries.dtype),
        in_specs=[smem] + in_vmem(4),
        out_specs=pl.BlockSpec(memory_space=pltpu.VMEM),
        name="finish",
    )(clip_tokens, attended, squares, sum(others), factor)


def passed_along(shard, axis, by):
    peers = lax.axis_size(axis)
    pairs = [(i, i + by) for i in range(peers) if 0 <= i + by < peers]
    return lax.ppermute(shard, axis, pairs)


def by_blocks(queries, keys_values, clip_tokens, noise_level, level_gate, out_gain):
    tokens_here = queries.shape[1]
    slot_count = tokens_here * lax.axis_size("seq")
    clip_count = clip_tokens.shape[0]
    kv_heads_here = keys_values.shape[-1] // HD
    heads_here = queries.shape[-1] // HD
    group_size = heads_here // kv_heads_here
    own_clip = lax.axis_index("span")
    own_seq = lax.axis_index("seq")
    query_heads = queries[0].reshape(tokens_here, kv_heads_here, group_size, HD)
    score_scale = 1.0 / math.sqrt(HD)
    clip_ids = jnp.arange(clip_count, dtype=jnp.int32)

    def clip_length(which):
        return jnp.sum(
            jnp.where(which[:, None] == clip_ids[None, :], clip_tokens[None, :], 0), axis=1
        )

    def block_step(running, key_block, first):
        key_count = key_block.shape[1]
        positions = first + jnp.arange(key_count, dtype=jnp.int32)
        holder = positions // slot_count
        slot_index = positions - holder * slot_count
        usable = (holder >= 0) & (holder <= own_clip) & (slot_index < clip_length(holder))

        def update(state):
            running_max, weight_sum, weighted = state
            key_rows = key_block[0].reshape(key_count, kv_heads_here, HD)
            value_rows = key_block[1].reshape(key_count, kv_heads_here, HD)
            scores = (
                jnp.einsum(
                    "tgrd,kgd->tgrk", query_heads, key_rows, preferred_element_type=jnp.float32
                )
                * score_scale
            )
            scores = jnp.where(usable[None, None, None, :], scores, -jnp.inf)
            new_max = jnp.maximum(running_max, jnp.max(scores, axis=-1))
            weights = jnp.exp(scores - new_max[..., None])
            shrink = jnp.exp(running_max - new_max)
            weight_sum = weight_sum * shrink + jnp.sum(weights, axis=-1)
            weighted = weighted * shrink[..., None] + jnp.einsum(
                "tgrk,kgd->tgrd",
                weights.astype(jnp.bfloat16),
                value_rows,
                preferred_element_type=jnp.float32,
            )
            return (new_max, weight_sum, weighted)

        def unchanged(state):
            return state

        return lax.cond(jnp.any(usable), update, unchanged, running)

    def fold_piece(running, kv_piece, first):
        key_count = kv_piece.shape[1]
        if key_count > 1024 and key_count % 1024 == 0:

            def loop_step(block_index, state):
                key_block = lax.dynamic_slice_in_dim(kv_piece, block_index * 1024, 1024, 1)
                return block_step(state, key_block, first + block_index * 1024)

            return lax.fori_loop(0, key_count // 1024, loop_step, running)
        return block_step(running, kv_piece, first)

    initial = (
        jnp.full((tokens_here, kv_heads_here, group_size), -jnp.inf, jnp.float32),
        jnp.zeros((tokens_here, kv_heads_here, group_size), jnp.float32),
        jnp.zeros((tokens_here, kv_heads_here, group_size, HD), jnp.float32),
    )
    local_kv = keys_values[:, 0]
    clip_kv = lax.all_gather(local_kv, "seq", axis=1, tiled=True)
    running = fold_piece(initial, clip_kv, own_clip * slot_count)
    for distance in range(1, clip_count):
        clip_kv = passed_along(clip_kv, "span", 1)
        running = fold_piece(running, clip_kv, (own_clip - distance) * slot_count)
    running_max, weight_sum, weighted = running
    attended = (weighted / weight_sum[..., None]).reshape(
        tokens_here, kv_heads_here * group_size * HD
    )
    squares = jnp.sum(attended * attended, axis=1)
    mean_square = lax.psum(squares, "mp") / (heads_here * HD * lax.axis_size("mp"))
    own_level = jnp.sum(jnp.where(clip_ids == own_clip, noise_level, 0))
    one_hot = (jnp.arange(level_gate.shape[0], dtype=jnp.int32) == own_level).astype(jnp.bfloat16)
    gate_row = jnp.dot(one_hot, level_gate, preferred_element_type=jnp.float32)
    own_length = jnp.sum(jnp.where(clip_ids == own_clip, clip_tokens, 0))
    usable_rows = own_seq * tokens_here + jnp.arange(tokens_here, dtype=jnp.int32) < own_length
    normed = (
        attended
        * lax.rsqrt(mean_square + 1e-06)[:, None]
        * out_gain.astype(jnp.float32)
        * (1.0 + gate_row)
    )
    return jnp.where(usable_rows[:, None], normed, 0.0).astype(jnp.bfloat16)[None]


def per_device(*arrays):
    few = all(lax.axis_size(axis) in (2, 4) for axis in ("span", "seq")) and lax.axis_size("mp") == 2
    return (by_exchange if few else by_blocks)(*arrays)


def solution(mesh):
    placed = (
        P("span", "seq", "mp"),
        P(None, "span", "seq", "mp"),
        P(),
        P(),
        P(None, "mp"),
        P("mp"),
    )
    return jax.shard_map(
        per_device, mesh=mesh, in_specs=placed, out_specs=P("span", "seq", "mp"), check_vma=False
    )
```

```python
import functools
import math

import jax
import jax.numpy as jnp
from jax import lax
from jax.experimental import pallas as pl
from jax.experimental.pallas import tpu as pltpu
from jax.sharding import PartitionSpec as P

HD = 128
MASKED = -1e30


def exchanged(shard, axis, by):
    peers = lax.axis_size(axis)
    return lax.ppermute(shard, axis, [(i, i ^ by) for i in range(peers)])


def in_vmem(count):
    return [pl.BlockSpec(memory_space=pltpu.VMEM)] * count


def in_hbm(array):
    return pltpu.with_memory_space_constraint(array, pltpu.HBM)


def gate_factor(level, gate_ref, gain_ref):
    levels = gate_ref.shape[0]
    one_hot = (lax.broadcasted_iota(jnp.int32, (16, levels), 1) == level).astype(jnp.bfloat16)
    row = jnp.dot(one_hot, gate_ref[...], preferred_element_type=jnp.float32)[:8]
    gain = gain_ref[...].astype(jnp.float32)
    return jnp.broadcast_to(gain[None, :], row.shape) * (1.0 + row)


def prepare_kernel(offsets, count, *refs):
    sources, outs, (arrived,) = refs[:6], refs[6 : 6 + count], refs[-1:]
    rows_ref, own_ref, factor_ref, bias_ref, live_ref = outs
    scratch = refs[6 + count : -1]
    q_ref, gate_ref, gain_ref, tokens_ref, level_ref = scratch
    places = (q_ref, gate_ref, gain_ref, tokens_ref, level_ref, own_ref)
    copies = [
        pltpu.make_async_copy(src, dst, arrived.at[i])
        for i, (src, dst) in enumerate(zip(sources, places))
    ]
    for copy in copies:
        copy.start()
    copies[0].wait()
    kv_heads, stacked = rows_ref.shape[:2]
    rows = q_ref.shape[0]
    group_size = stacked // rows
    for g in range(kv_heads):
        for r in range(group_size):
            h = g * group_size + r
            rows_ref[g, r * rows : (r + 1) * rows] = q_ref[:, h * HD : (h + 1) * HD]
    for copy in copies[1:]:
        copy.wait()
    own_clip = lax.axis_index("span")
    own_seq = lax.axis_index("seq")
    factor_ref[...] = gate_factor(level_ref[own_clip], gate_ref, gain_ref)
    lane = lax.broadcasted_iota(jnp.int32, (8, rows), 1)
    biases = []
    for clip_by, seq_by in offsets:
        clip = own_clip ^ clip_by
        live = tokens_ref[clip] - (own_seq ^ seq_by) * rows
        biases.append(jnp.where(lane < jnp.where(clip <= own_clip, live, 0), 0.0, MASKED))
    bias_ref[...] = jnp.concatenate(biases, axis=1)
    slot = own_seq * rows + lax.broadcasted_iota(jnp.int32, live_ref.shape, 0)
    live_ref[...] = (slot < tokens_ref[own_clip]).astype(jnp.float32)


def fold(query_rows, kv_refs, bias, lanes, state):
    to_exponent = math.log2(math.e) / math.sqrt(HD)
    key_rows = jnp.concatenate([ref[0, :, lanes] for ref in kv_refs], axis=0)
    value_rows = jnp.concatenate([ref[1, :, lanes] for ref in kv_refs], axis=0)
    scores = lax.dot_general(
        query_rows, key_rows, (((1,), (1,)), ((), ())), preferred_element_type=jnp.float32
    )
    scores = scores + bias
    tiles = [slice(i, i + HD) for i in range(0, scores.shape[1], HD)]
    highest = functools.reduce(jnp.maximum, [scores[:, tile] for tile in tiles])
    if state is not None:
        highest = jnp.maximum(highest, state[0])
    new_max = jnp.max(highest, axis=1, keepdims=True)
    weights = jnp.exp2((scores - new_max) * to_exponent)
    weight_sums = functools.reduce(jnp.add, [weights[:, tile] for tile in tiles])
    mixed = jnp.dot(weights.astype(jnp.bfloat16), value_rows, preferred_element_type=jnp.float32)
    if state is not None:
        shrink = jnp.exp2((state[0] - new_max) * to_exponent)
        weight_sums = weight_sums + state[1] * shrink
        mixed = mixed + state[2] * shrink
    return new_max, weight_sums, mixed


def early_kernel(rows_ref, bias_ref, *refs):
    kv_refs, (max_ref, sums_ref, mixed_ref) = refs[:-3], refs[-3:]
    keys = kv_refs[0].shape[1] * len(kv_refs)
    for g in range(rows_ref.shape[0]):
        lanes = slice(g * HD, (g + 1) * HD)
        state = fold(rows_ref[g], kv_refs, bias_ref[0:1, :keys], lanes, None)
        max_ref[g] = jnp.broadcast_to(state[0], max_ref.shape[1:])
        sums_ref[g] = state[1]
        mixed_ref[g] = state[2]


def late_kernel(group_size, rows_ref, bias_ref, *refs):
    states, kv_refs, (attended_ref, squares_ref) = refs[:3], refs[3:-2], refs[-2:]
    rows = rows_ref.shape[1] // group_size
    first = bias_ref.shape[1] - kv_refs[0].shape[1] * len(kv_refs)
    squares = jnp.zeros((rows, HD), jnp.float32)
    for g in range(rows_ref.shape[0]):
        lanes = slice(g * HD, (g + 1) * HD)
        state = [ref[g] for ref in states]
        _, weight_sums, mixed = fold(rows_ref[g], kv_refs, bias_ref[0:1, first:], lanes, state)
        mixed = mixed / jnp.sum(weight_sums, axis=1, keepdims=True)
        for r in range(group_size):
            block = mixed[r * rows : (r + 1) * rows]
            h = g * group_size + r
            attended_ref[:, h * HD : (h + 1) * HD] = block
            squares = squares + block * block
    squares_ref[...] = jnp.sum(squares.T, axis=0, keepdims=True)


def finish_kernel(features, attended_ref, own_ref, other_ref, factor_ref, live_ref, out_ref):
    rows = attended_ref.shape[0]
    mean_square = (own_ref[...] + other_ref[...]) / features
    scale = jnp.broadcast_to(lax.rsqrt(mean_square + 1e-06), (HD, rows)).T
    live = live_ref[...] > 0.0
    for h in range(attended_ref.shape[1] // HD):
        lanes = slice(h * HD, (h + 1) * HD)
        block = attended_ref[:, lanes] * scale * factor_ref[0:1, lanes]
        out_ref[0, :, lanes] = jnp.where(live, block, 0.0).astype(out_ref.dtype)


def kernel(body, outs, count, megabytes, name):
    several = isinstance(outs, tuple)
    return pl.pallas_call(
        body,
        out_shape=outs,
        in_specs=in_vmem(count),
        out_specs=tuple(in_vmem(len(outs))) if several else in_vmem(1)[0],
        compiler_params=pltpu.CompilerParams(vmem_limit_bytes=megabytes * 1024 * 1024),
        name=name,
    )


def after(array, *others):
    return lax.optimization_barrier((array, *others))[0]


def arrival_order():
    clips, parts = lax.axis_size("span"), lax.axis_size("seq")
    across = clips // 2
    late = [(by, at) for at in range(1, max(parts // 2, 1) + 1) for by in range(across, clips)]
    early = [(by, at) for by in range(clips) for at in range(parts)]
    return [at for at in early if at not in late], late


def travel(own, prepared):
    pieces = {(0, 0): own}
    far_first = range(lax.axis_size("seq") - 1, 0, -1)
    for seq_by in far_first:
        pieces[0, seq_by] = exchanged(own, "seq", seq_by)
    across = lax.axis_size("span") // 2
    for seq_by in (0, *far_first):
        piece = pieces[0, seq_by]
        if seq_by == far_first[1 if len(far_first) > 1 else 0]:
            piece = after(piece, prepared)
        pieces[across, seq_by] = exchanged(piece, "span", across)
        if across > 1:
            pieces[1, seq_by] = exchanged(pieces[0, seq_by], "span", 1)
    if across > 1:
        for seq_by in (0, *far_first):
            pieces[across + 1, seq_by] = exchanged(pieces[across, seq_by], "span", 1)
    return pieces


def by_exchange(queries, keys_values, clip_tokens, noise_level, level_gate, out_gain):
    tokens_here, width = queries.shape[1:]
    kv_heads_here = keys_values.shape[-1] // HD
    group_size = width // HD // kv_heads_here
    own = keys_values[:, 0]
    f32 = functools.partial(jax.ShapeDtypeStruct, dtype=jnp.float32)
    stacked = (kv_heads_here, group_size * tokens_here, HD)
    early, late = arrival_order()
    outs = (
        jax.ShapeDtypeStruct(stacked, queries.dtype),
        jax.ShapeDtypeStruct(own.shape, own.dtype),
        f32((8, width)),
        f32((8, tokens_here * len(early + late))),
        f32((tokens_here, HD)),
    )
    sources = (queries[0], level_gate, out_gain, clip_tokens, noise_level, own)
    spaces = (pltpu.VMEM, pltpu.VMEM, pltpu.VMEM, pltpu.SMEM, pltpu.SMEM)
    rows, own_kept, factor, bias, live = pl.pallas_call(
        functools.partial(prepare_kernel, early + late, len(outs)),
        out_shape=outs,
        in_specs=[pl.BlockSpec(memory_space=pltpu.HBM)] * len(sources),
        out_specs=tuple(in_vmem(len(outs))),
        scratch_shapes=[space(x.shape, x.dtype) for space, x in zip(spaces, sources)]
        + [pltpu.SemaphoreType.DMA((len(sources),))],
        compiler_params=pltpu.CompilerParams(vmem_limit_bytes=8 * 1024 * 1024),
        name="prepare",
    )(*(in_hbm(x) for x in sources))
    pieces = travel(own, rows)
    pieces[0, 0] = own_kept
    state = kernel(early_kernel, (f32(stacked),) * 3, 2 + len(early), 16, "attend_early")(
        rows, bias, *[pieces[at] for at in early]
    )
    attended, squares = kernel(
        functools.partial(late_kernel, group_size),
        (f32((tokens_here, width)), f32((1, tokens_here))),
        5 + len(late), 16, "attend_late",
    )(rows, bias, *state, *[pieces[at] for at in late])
    others = [exchanged(squares, "mp", by) for by in range(1, lax.axis_size("mp"))]
    return kernel(
        functools.partial(finish_kernel, width * lax.axis_size("mp")),
        jax.ShapeDtypeStruct(queries.shape, queries.dtype),
        5, 4, "finish",
    )(attended, squares, sum(others), factor, live)


def passed_along(shard, axis, by):
    peers = lax.axis_size(axis)
    pairs = [(i, i + by) for i in range(peers) if 0 <= i + by < peers]
    return lax.ppermute(shard, axis, pairs)


def by_blocks(queries, keys_values, clip_tokens, noise_level, level_gate, out_gain):
    tokens_here = queries.shape[1]
    slot_count = tokens_here * lax.axis_size("seq")
    clip_count = clip_tokens.shape[0]
    kv_heads_here = keys_values.shape[-1] // HD
    heads_here = queries.shape[-1] // HD
    group_size = heads_here // kv_heads_here
    own_clip = lax.axis_index("span")
    own_seq = lax.axis_index("seq")
    query_heads = queries[0].reshape(tokens_here, kv_heads_here, group_size, HD)
    score_scale = 1.0 / math.sqrt(HD)
    clip_ids = jnp.arange(clip_count, dtype=jnp.int32)

    def clip_length(which):
        return jnp.sum(
            jnp.where(which[:, None] == clip_ids[None, :], clip_tokens[None, :], 0), axis=1
        )

    def block_step(running, key_block, first):
        key_count = key_block.shape[1]
        positions = first + jnp.arange(key_count, dtype=jnp.int32)
        holder = positions // slot_count
        slot_index = positions - holder * slot_count
        usable = (holder >= 0) & (holder <= own_clip) & (slot_index < clip_length(holder))

        def update(state):
            running_max, weight_sum, weighted = state
            key_rows = key_block[0].reshape(key_count, kv_heads_here, HD)
            value_rows = key_block[1].reshape(key_count, kv_heads_here, HD)
            scores = (
                jnp.einsum(
                    "tgrd,kgd->tgrk", query_heads, key_rows, preferred_element_type=jnp.float32
                )
                * score_scale
            )
            scores = jnp.where(usable[None, None, None, :], scores, -jnp.inf)
            new_max = jnp.maximum(running_max, jnp.max(scores, axis=-1))
            weights = jnp.exp(scores - new_max[..., None])
            shrink = jnp.exp(running_max - new_max)
            weight_sum = weight_sum * shrink + jnp.sum(weights, axis=-1)
            weighted = weighted * shrink[..., None] + jnp.einsum(
                "tgrk,kgd->tgrd",
                weights.astype(jnp.bfloat16),
                value_rows,
                preferred_element_type=jnp.float32,
            )
            return (new_max, weight_sum, weighted)

        def unchanged(state):
            return state

        return lax.cond(jnp.any(usable), update, unchanged, running)

    def fold_piece(running, kv_piece, first):
        key_count = kv_piece.shape[1]
        if key_count > 1024 and key_count % 1024 == 0:

            def loop_step(block_index, state):
                key_block = lax.dynamic_slice_in_dim(kv_piece, block_index * 1024, 1024, 1)
                return block_step(state, key_block, first + block_index * 1024)

            return lax.fori_loop(0, key_count // 1024, loop_step, running)
        return block_step(running, kv_piece, first)

    initial = (
        jnp.full((tokens_here, kv_heads_here, group_size), -jnp.inf, jnp.float32),
        jnp.zeros((tokens_here, kv_heads_here, group_size), jnp.float32),
        jnp.zeros((tokens_here, kv_heads_here, group_size, HD), jnp.float32),
    )
    local_kv = keys_values[:, 0]
    clip_kv = lax.all_gather(local_kv, "seq", axis=1, tiled=True)
    running = fold_piece(initial, clip_kv, own_clip * slot_count)
    for distance in range(1, clip_count):
        clip_kv = passed_along(clip_kv, "span", 1)
        running = fold_piece(running, clip_kv, (own_clip - distance) * slot_count)
    running_max, weight_sum, weighted = running
    attended = (weighted / weight_sum[..., None]).reshape(
        tokens_here, kv_heads_here * group_size * HD
    )
    squares = jnp.sum(attended * attended, axis=1)
    mean_square = lax.psum(squares, "mp") / (heads_here * HD * lax.axis_size("mp"))
    own_level = jnp.sum(jnp.where(clip_ids == own_clip, noise_level, 0))
    one_hot = (jnp.arange(level_gate.shape[0], dtype=jnp.int32) == own_level).astype(jnp.bfloat16)
    gate_row = jnp.dot(one_hot, level_gate, preferred_element_type=jnp.float32)
    own_length = jnp.sum(jnp.where(clip_ids == own_clip, clip_tokens, 0))
    usable_rows = own_seq * tokens_here + jnp.arange(tokens_here, dtype=jnp.int32) < own_length
    normed = (
        attended
        * lax.rsqrt(mean_square + 1e-06)[:, None]
        * out_gain.astype(jnp.float32)
        * (1.0 + gate_row)
    )
    return jnp.where(usable_rows[:, None], normed, 0.0).astype(jnp.bfloat16)[None]


def per_device(*arrays):
    few = all(lax.axis_size(axis) in (2, 4) for axis in ("span", "seq")) and lax.axis_size("mp") == 2
    return (by_exchange if few else by_blocks)(*arrays)


def solution(mesh):
    placed = (
        P("span", "seq", "mp"),
        P(None, "span", "seq", "mp"),
        P(),
        P(),
        P(None, "mp"),
        P("mp"),
    )
    return jax.shard_map(
        per_device, mesh=mesh, in_specs=placed, out_specs=P("span", "seq", "mp"), check_vma=False
    )
```

```python
import functools
import itertools
import math

import jax
import jax.numpy as jnp
from jax import lax
from jax.experimental import pallas as pl
from jax.experimental.pallas import tpu as pltpu
from jax.sharding import PartitionSpec as P

HD = 128
MASKED = -1e30
PREPARED = "prepared"


def plan_of():
    steps = [("p3", (0, 3), "own", None), ("p2", (0, 2), "own", None), ("p1", (0, 1), "own", None)]
    for part in "0321":
        source = "own" if part == "0" else "p" + part
        steps.append(("x" + part, (2, 0), source, PREPARED if part == "2" else None))
        steps.append(("c" + part, (1, 0), source, None))
    steps += [("d" + part, (1, 0), "x" + part, None) for part in "0321"]
    early = ["kept", "p1", "p2", "p3", "c0", "c1", "c2", "c3", "x0", "x3", "d0", "d3"]
    return steps, early, ["x1", "d1", "x2", "d2"]


def exchanged(shard, axes, by):
    sizes = [lax.axis_size(axis) for axis in axes]
    places = list(itertools.product(*(range(size) for size in sizes)))
    to = [tuple(i ^ k for i, k in zip(place, by)) for place in places]
    return lax.ppermute(shard, axes, [(i, places.index(there)) for i, there in enumerate(to)])


def in_vmem(count):
    return [pl.BlockSpec(memory_space=pltpu.VMEM)] * count


def in_hbm(array):
    return pltpu.with_memory_space_constraint(array, pltpu.HBM)


def gate_factor(level, gate_ref, gain_ref):
    levels = gate_ref.shape[0]
    one_hot = (lax.broadcasted_iota(jnp.int32, (16, levels), 1) == level).astype(jnp.bfloat16)
    row = jnp.dot(one_hot, gate_ref[...], preferred_element_type=jnp.float32)[:8]
    gain = gain_ref[...].astype(jnp.float32)
    return jnp.broadcast_to(gain[None, :], row.shape) * (1.0 + row)


def prepare_kernel(offsets, count, *refs):
    sources, outs, (arrived,) = refs[:6], refs[6 : 6 + count], refs[-1:]
    rows_ref, own_ref, factor_ref, bias_ref, live_ref = outs
    scratch = refs[6 + count : -1]
    q_ref, gate_ref, gain_ref, tokens_ref, level_ref = scratch
    places = (q_ref, gate_ref, gain_ref, tokens_ref, level_ref, own_ref)
    copies = [
        pltpu.make_async_copy(src, dst, arrived.at[i])
        for i, (src, dst) in enumerate(zip(sources, places))
    ]
    for copy in copies:
        copy.start()
    copies[0].wait()
    kv_heads, stacked = rows_ref.shape[:2]
    rows = q_ref.shape[0]
    group_size = stacked // rows
    for g in range(kv_heads):
        for r in range(group_size):
            h = g * group_size + r
            rows_ref[g, r * rows : (r + 1) * rows] = q_ref[:, h * HD : (h + 1) * HD]
    for copy in copies[1:]:
        copy.wait()
    own_clip = lax.axis_index("span")
    own_seq = lax.axis_index("seq")
    factor_ref[...] = gate_factor(level_ref[own_clip], gate_ref, gain_ref)
    lane = lax.broadcasted_iota(jnp.int32, (8, rows), 1)
    biases = []
    for clip_by, seq_by in offsets:
        clip = own_clip ^ clip_by
        live = tokens_ref[clip] - (own_seq ^ seq_by) * rows
        biases.append(jnp.where(lane < jnp.where(clip <= own_clip, live, 0), 0.0, MASKED))
    bias_ref[...] = jnp.concatenate(biases, axis=1)
    slot = own_seq * rows + lax.broadcasted_iota(jnp.int32, live_ref.shape, 0)
    live_ref[...] = (slot < tokens_ref[own_clip]).astype(jnp.float32)


def fold(query_rows, kv_refs, bias, lanes, state):
    to_exponent = math.log2(math.e) / math.sqrt(HD)
    pieces = [(ref, i) for ref in kv_refs for i in range(ref.shape[0])]
    key_rows = jnp.concatenate([ref[i, 0, :, lanes] for ref, i in pieces], axis=0)
    value_rows = jnp.concatenate([ref[i, 1, :, lanes] for ref, i in pieces], axis=0)
    scores = lax.dot_general(
        query_rows, key_rows, (((1,), (1,)), ((), ())), preferred_element_type=jnp.float32
    )
    scores = scores + bias
    tiles = [slice(i, i + HD) for i in range(0, scores.shape[1], HD)]
    highest = functools.reduce(jnp.maximum, [scores[:, tile] for tile in tiles])
    if state is not None:
        highest = jnp.maximum(highest, state[0])
    new_max = jnp.max(highest, axis=1, keepdims=True)
    weights = jnp.exp2((scores - new_max) * to_exponent)
    weight_sums = functools.reduce(jnp.add, [weights[:, tile] for tile in tiles])
    mixed = jnp.dot(weights.astype(jnp.bfloat16), value_rows, preferred_element_type=jnp.float32)
    if state is not None:
        shrink = jnp.exp2((state[0] - new_max) * to_exponent)
        weight_sums = weight_sums + state[1] * shrink
        mixed = mixed + state[2] * shrink
    return new_max, weight_sums, mixed


def keys_in(kv_refs):
    return sum(ref.shape[0] * ref.shape[2] for ref in kv_refs)


def upper_clips():
    return lax.axis_index("span") >= lax.axis_size("span") // 2


def early_kernel(lower_count, rows_ref, bias_ref, *refs):
    kv_refs, (max_ref, sums_ref, mixed_ref) = refs[:-3], refs[-3:]

    def fold_in(kv_refs):
        keys = keys_in(kv_refs)
        for g in range(rows_ref.shape[0]):
            lanes = slice(g * HD, (g + 1) * HD)
            state = fold(rows_ref[g], kv_refs, bias_ref[0:1, :keys], lanes, None)
            max_ref[g] = jnp.broadcast_to(state[0], max_ref.shape[1:])
            sums_ref[g] = state[1]
            mixed_ref[g] = state[2]

    pl.when(upper_clips())(lambda: fold_in(kv_refs))
    pl.when(jnp.logical_not(upper_clips()))(lambda: fold_in(kv_refs[:lower_count]))


def late_kernel(group_size, rows_ref, bias_ref, *refs):
    states, kv_refs, (attended_ref, squares_ref) = refs[:3], refs[3:-2], refs[-2:]
    rows = rows_ref.shape[1] // group_size
    first = bias_ref.shape[1] - keys_in(kv_refs)

    def end(folds):
        squares = jnp.zeros((rows, HD), jnp.float32)
        for g in range(rows_ref.shape[0]):
            lanes = slice(g * HD, (g + 1) * HD)
            state = [ref[g] for ref in states]
            if folds:
                state = fold(rows_ref[g], kv_refs, bias_ref[0:1, first:], lanes, state)
            mixed = state[2] / jnp.sum(state[1], axis=1, keepdims=True)
            for r in range(group_size):
                block = mixed[r * rows : (r + 1) * rows]
                h = g * group_size + r
                attended_ref[:, h * HD : (h + 1) * HD] = block
                squares = squares + block * block
        squares_ref[...] = jnp.sum(squares.T, axis=0, keepdims=True)

    pl.when(upper_clips())(lambda: end(True))
    pl.when(jnp.logical_not(upper_clips()))(lambda: end(False))


def finish_kernel(features, attended_ref, own_ref, other_ref, factor_ref, live_ref, out_ref):
    rows = attended_ref.shape[0]
    mean_square = (own_ref[...] + other_ref[...]) / features
    scale = jnp.broadcast_to(lax.rsqrt(mean_square + 1e-06), (HD, rows)).T
    live = live_ref[...] > 0.0
    for h in range(attended_ref.shape[1] // HD):
        lanes = slice(h * HD, (h + 1) * HD)
        block = attended_ref[:, lanes] * scale * factor_ref[0:1, lanes]
        out_ref[0, :, lanes] = jnp.where(live, block, 0.0).astype(out_ref.dtype)


def kernel(body, outs, count, megabytes, name):
    several = isinstance(outs, tuple)
    return pl.pallas_call(
        body,
        out_shape=outs,
        in_specs=in_vmem(count),
        out_specs=tuple(in_vmem(len(outs))) if several else in_vmem(1)[0],
        compiler_params=pltpu.CompilerParams(vmem_limit_bytes=megabytes * 1024 * 1024),
        name=name,
    )


def after(array, *others):
    return lax.optimization_barrier((array, *others))[0]


def offsets_of(steps):
    at = {"own": [(0, 0)], "kept": [(0, 0)]}
    for name, hop, source, _ in steps:
        if hop is None:
            at[name] = [offset for part in source for offset in at[part]]
        else:
            at[name] = [(clip ^ hop[0], part ^ hop[1]) for clip, part in at[source]]
    return at


def pack_kernel(*refs):
    at = 0
    for ref in refs[:-1]:
        refs[-1][at : at + ref.shape[0]] = ref[...]
        at += ref.shape[0]


def pack(arrays):
    shape = (sum(array.shape[0] for array in arrays), *arrays[0].shape[1:])
    out = jax.ShapeDtypeStruct(shape, arrays[0].dtype)
    return kernel(pack_kernel, out, len(arrays), 4, "pack")(*arrays)


def travel(steps, own, kept, prepared):
    have = {"own": own, "kept": kept, PREPARED: prepared}
    for name, hop, source, wait_for in steps:
        if hop is None:
            have[name] = pack([have[part] for part in source])
        else:
            shard = have[source]
            if wait_for is not None:
                shard = after(shard, *[have[n] for n in wait_for.split()])
            have[name] = exchanged(shard, ("span", "seq"), hop)
    return have


def by_exchange(queries, keys_values, clip_tokens, noise_level, level_gate, out_gain):
    tokens_here, width = queries.shape[1:]
    kv_heads_here = keys_values.shape[-1] // HD
    group_size = width // HD // kv_heads_here
    own = keys_values[None, :, 0]
    f32 = functools.partial(jax.ShapeDtypeStruct, dtype=jnp.float32)
    stacked = (kv_heads_here, group_size * tokens_here, HD)
    steps, early, late = plan_of()
    offsets = offsets_of(steps)
    across = lax.axis_size("span") // 2
    lower_count = sum(all(by < across for by, _ in offsets[name]) for name in early)
    offsets = [at for name in early + late for at in offsets[name]]
    outs = (
        jax.ShapeDtypeStruct(stacked, queries.dtype),
        jax.ShapeDtypeStruct(own.shape, own.dtype),
        f32((8, width)),
        f32((8, tokens_here * len(offsets))),
        f32((tokens_here, HD)),
    )
    sources = (queries[0], level_gate, out_gain, clip_tokens, noise_level, own)
    spaces = (pltpu.VMEM, pltpu.VMEM, pltpu.VMEM, pltpu.SMEM, pltpu.SMEM)
    rows, own_kept, factor, bias, live = pl.pallas_call(
        functools.partial(prepare_kernel, offsets, len(outs)),
        out_shape=outs,
        in_specs=[pl.BlockSpec(memory_space=pltpu.HBM)] * len(sources),
        out_specs=tuple(in_vmem(len(outs))),
        scratch_shapes=[space(x.shape, x.dtype) for space, x in zip(spaces, sources)]
        + [pltpu.SemaphoreType.DMA((len(sources),))],
        compiler_params=pltpu.CompilerParams(vmem_limit_bytes=8 * 1024 * 1024),
        name="prepare",
    )(*(in_hbm(x) for x in sources))
    have = travel(steps, own, own_kept, rows)
    state = kernel(
        functools.partial(early_kernel, lower_count), (f32(stacked),) * 3, 2 + len(early), 16, "attend_early"
    )(
        rows, bias, *[have[name] for name in early]
    )
    attended, squares = kernel(
        functools.partial(late_kernel, group_size),
        (f32((tokens_here, width)), f32((1, tokens_here))),
        5 + len(late), 16, "attend_late",
    )(rows, bias, *state, *[have[name] for name in late])
    others = [exchanged(squares, ("mp",), (by,)) for by in range(1, lax.axis_size("mp"))]
    return kernel(
        functools.partial(finish_kernel, width * lax.axis_size("mp")),
        jax.ShapeDtypeStruct(queries.shape, queries.dtype),
        5, 4, "finish",
    )(attended, squares, sum(others), factor, live)


def passed_along(shard, axis, by):
    peers = lax.axis_size(axis)
    pairs = [(i, i + by) for i in range(peers) if 0 <= i + by < peers]
    return lax.ppermute(shard, axis, pairs)


def by_blocks(queries, keys_values, clip_tokens, noise_level, level_gate, out_gain):
    tokens_here = queries.shape[1]
    slot_count = tokens_here * lax.axis_size("seq")
    clip_count = clip_tokens.shape[0]
    kv_heads_here = keys_values.shape[-1] // HD
    heads_here = queries.shape[-1] // HD
    group_size = heads_here // kv_heads_here
    own_clip = lax.axis_index("span")
    own_seq = lax.axis_index("seq")
    query_heads = queries[0].reshape(tokens_here, kv_heads_here, group_size, HD)
    score_scale = 1.0 / math.sqrt(HD)
    clip_ids = jnp.arange(clip_count, dtype=jnp.int32)

    def clip_length(which):
        return jnp.sum(
            jnp.where(which[:, None] == clip_ids[None, :], clip_tokens[None, :], 0), axis=1
        )

    def block_step(running, key_block, first):
        key_count = key_block.shape[1]
        positions = first + jnp.arange(key_count, dtype=jnp.int32)
        holder = positions // slot_count
        slot_index = positions - holder * slot_count
        usable = (holder >= 0) & (holder <= own_clip) & (slot_index < clip_length(holder))

        def update(state):
            running_max, weight_sum, weighted = state
            key_rows = key_block[0].reshape(key_count, kv_heads_here, HD)
            value_rows = key_block[1].reshape(key_count, kv_heads_here, HD)
            scores = (
                jnp.einsum(
                    "tgrd,kgd->tgrk", query_heads, key_rows, preferred_element_type=jnp.float32
                )
                * score_scale
            )
            scores = jnp.where(usable[None, None, None, :], scores, -jnp.inf)
            new_max = jnp.maximum(running_max, jnp.max(scores, axis=-1))
            weights = jnp.exp(scores - new_max[..., None])
            shrink = jnp.exp(running_max - new_max)
            weight_sum = weight_sum * shrink + jnp.sum(weights, axis=-1)
            weighted = weighted * shrink[..., None] + jnp.einsum(
                "tgrk,kgd->tgrd",
                weights.astype(jnp.bfloat16),
                value_rows,
                preferred_element_type=jnp.float32,
            )
            return (new_max, weight_sum, weighted)

        def unchanged(state):
            return state

        return lax.cond(jnp.any(usable), update, unchanged, running)

    def fold_piece(running, kv_piece, first):
        key_count = kv_piece.shape[1]
        if key_count > 1024 and key_count % 1024 == 0:

            def loop_step(block_index, state):
                key_block = lax.dynamic_slice_in_dim(kv_piece, block_index * 1024, 1024, 1)
                return block_step(state, key_block, first + block_index * 1024)

            return lax.fori_loop(0, key_count // 1024, loop_step, running)
        return block_step(running, kv_piece, first)

    initial = (
        jnp.full((tokens_here, kv_heads_here, group_size), -jnp.inf, jnp.float32),
        jnp.zeros((tokens_here, kv_heads_here, group_size), jnp.float32),
        jnp.zeros((tokens_here, kv_heads_here, group_size, HD), jnp.float32),
    )
    local_kv = keys_values[:, 0]
    clip_kv = lax.all_gather(local_kv, "seq", axis=1, tiled=True)
    running = fold_piece(initial, clip_kv, own_clip * slot_count)
    for distance in range(1, clip_count):
        clip_kv = passed_along(clip_kv, "span", 1)
        running = fold_piece(running, clip_kv, (own_clip - distance) * slot_count)
    running_max, weight_sum, weighted = running
    attended = (weighted / weight_sum[..., None]).reshape(
        tokens_here, kv_heads_here * group_size * HD
    )
    squares = jnp.sum(attended * attended, axis=1)
    mean_square = lax.psum(squares, "mp") / (heads_here * HD * lax.axis_size("mp"))
    own_level = jnp.sum(jnp.where(clip_ids == own_clip, noise_level, 0))
    one_hot = (jnp.arange(level_gate.shape[0], dtype=jnp.int32) == own_level).astype(jnp.bfloat16)
    gate_row = jnp.dot(one_hot, level_gate, preferred_element_type=jnp.float32)
    own_length = jnp.sum(jnp.where(clip_ids == own_clip, clip_tokens, 0))
    usable_rows = own_seq * tokens_here + jnp.arange(tokens_here, dtype=jnp.int32) < own_length
    normed = (
        attended
        * lax.rsqrt(mean_square + 1e-06)[:, None]
        * out_gain.astype(jnp.float32)
        * (1.0 + gate_row)
    )
    return jnp.where(usable_rows[:, None], normed, 0.0).astype(jnp.bfloat16)[None]


def per_device(*arrays):
    sizes = tuple(lax.axis_size(axis) for axis in ("span", "seq", "mp"))
    few = sizes == (4, 4, 2)
    return (by_exchange if few else by_blocks)(*arrays)


def solution(mesh):
    placed = (
        P("span", "seq", "mp"),
        P(None, "span", "seq", "mp"),
        P(),
        P(),
        P(None, "mp"),
        P("mp"),
    )
    return jax.shard_map(
        per_device, mesh=mesh, in_specs=placed, out_specs=P("span", "seq", "mp"), check_vma=False
    )
```

```python
import functools
import itertools
import math

import jax
import jax.numpy as jnp
from jax import lax
from jax.experimental import pallas as pl
from jax.experimental.pallas import tpu as pltpu
from jax.sharding import PartitionSpec as P

HD = 128
MASKED = -1e30
PREPARED = "prepared"


def plan_of():
    steps = [("p3", (0, 3), "own", None), ("p2", (0, 2), "own", None), ("p1", (0, 1), "own", None)]
    steps += [("x0", (2, 0), "own", None), ("c0", (1, 0), "own", PREPARED)]
    steps += [("x3", (2, 0), "p3", None), ("x2", (2, 0), "p2", None)]
    steps += [("c3", (1, 0), "p3", None), ("c2", (1, 0), "p2", None)]
    steps += [("x1", (2, 0), "p1", None), ("c1", (1, 0), "p1", None)]
    steps += [("d" + part, (1, 0), "x" + part, None) for part in "0321"]
    early = ["kept", "p3", "p2", "c2", "c0", "c1", "p1", "c3", "x1", "x3", "d3", "d0"]
    return steps, early, ["d2", "d1", "x2", "x0"]


def exchanged(shard, axes, by):
    sizes = [lax.axis_size(axis) for axis in axes]
    places = list(itertools.product(*(range(size) for size in sizes)))
    to = [tuple(i ^ k for i, k in zip(place, by)) for place in places]
    return lax.ppermute(shard, axes, [(i, places.index(there)) for i, there in enumerate(to)])


def in_vmem(count):
    return [pl.BlockSpec(memory_space=pltpu.VMEM)] * count


def in_hbm(array):
    return pltpu.with_memory_space_constraint(array, pltpu.HBM)


def gate_factor(level, gate_ref, gain_ref):
    levels = gate_ref.shape[0]
    one_hot = (lax.broadcasted_iota(jnp.int32, (16, levels), 1) == level).astype(jnp.bfloat16)
    row = jnp.dot(one_hot, gate_ref[...], preferred_element_type=jnp.float32)[:8]
    gain = gain_ref[...].astype(jnp.float32)
    return jnp.broadcast_to(gain[None, :], row.shape) * (1.0 + row)


def prepare_kernel(offsets, count, *refs):
    sources, outs, (arrived,) = refs[:6], refs[6 : 6 + count], refs[-1:]
    rows_ref, own_ref, factor_ref, bias_ref, live_ref = outs
    scratch = refs[6 + count : -1]
    q_ref, gate_ref, gain_ref, tokens_ref, level_ref = scratch
    places = (q_ref, gate_ref, gain_ref, tokens_ref, level_ref, own_ref)
    copies = [
        pltpu.make_async_copy(src, dst, arrived.at[i])
        for i, (src, dst) in enumerate(zip(sources, places))
    ]
    for copy in copies:
        copy.start()
    copies[0].wait()
    kv_heads, stacked = rows_ref.shape[:2]
    rows = q_ref.shape[0]
    group_size = stacked // rows
    for g in range(kv_heads):
        for r in range(group_size):
            h = g * group_size + r
            rows_ref[g, r * rows : (r + 1) * rows] = q_ref[:, h * HD : (h + 1) * HD]
    for copy in copies[1:]:
        copy.wait()
    own_clip = lax.axis_index("span")
    own_seq = lax.axis_index("seq")
    factor_ref[...] = gate_factor(level_ref[own_clip], gate_ref, gain_ref)
    lane = lax.broadcasted_iota(jnp.int32, (8, rows), 1)
    biases = []
    for clip_by, seq_by in offsets:
        clip = own_clip ^ clip_by
        live = tokens_ref[clip] - (own_seq ^ seq_by) * rows
        biases.append(jnp.where(lane < jnp.where(clip <= own_clip, live, 0), 0.0, MASKED))
    bias_ref[...] = jnp.concatenate(biases, axis=1)
    slot = own_seq * rows + lax.broadcasted_iota(jnp.int32, live_ref.shape, 0)
    live_ref[...] = (slot < tokens_ref[own_clip]).astype(jnp.float32)


def fold(query_rows, kv_refs, bias, lanes, state):
    to_exponent = math.log2(math.e) / math.sqrt(HD)
    pieces = [(ref, i) for ref in kv_refs for i in range(ref.shape[0])]
    key_rows = jnp.concatenate([ref[i, 0, :, lanes] for ref, i in pieces], axis=0)
    value_rows = jnp.concatenate([ref[i, 1, :, lanes] for ref, i in pieces], axis=0)
    scores = lax.dot_general(
        query_rows, key_rows, (((1,), (1,)), ((), ())), preferred_element_type=jnp.float32
    )
    scores = scores + bias
    tiles = [slice(i, i + HD) for i in range(0, scores.shape[1], HD)]
    highest = functools.reduce(jnp.maximum, [scores[:, tile] for tile in tiles])
    if state is not None:
        highest = jnp.maximum(highest, state[0])
    new_max = jnp.max(highest, axis=1, keepdims=True)
    weights = jnp.exp2((scores - new_max) * to_exponent)
    weight_sums = functools.reduce(jnp.add, [weights[:, tile] for tile in tiles])
    mixed = jnp.dot(weights.astype(jnp.bfloat16), value_rows, preferred_element_type=jnp.float32)
    if state is not None:
        shrink = jnp.exp2((state[0] - new_max) * to_exponent)
        weight_sums = weight_sums + state[1] * shrink
        mixed = mixed + state[2] * shrink
    return new_max, weight_sums, mixed


def keys_in(kv_refs):
    return sum(ref.shape[0] * ref.shape[2] for ref in kv_refs)


def on_half(offsets, counts, call):
    across = lax.axis_size("span") // 2
    upper = lax.axis_index("span") >= across
    useful, at = [], 0
    for i, count in enumerate(counts):
        if any(by < across for by, _ in offsets[at : at + count]):
            useful.append(i)
        at += count
    while sum(counts[i] for i in useful) % 2:
        useful.append(min(i for i in range(len(counts)) if i not in useful))
    pl.when(upper)(lambda: call(list(range(len(counts)))))
    pl.when(jnp.logical_not(upper))(lambda: call(useful))


def bias_of(bias_ref, first, kv_refs, chosen):
    parts, at = [], first
    for i, ref in enumerate(kv_refs):
        if i in chosen:
            parts.append(bias_ref[0:1, at : at + keys_in([ref])])
        at += keys_in([ref])
    return jnp.concatenate(parts, axis=1)


def early_kernel(offsets, rows_ref, bias_ref, *refs):
    kv_refs, (max_ref, sums_ref, mixed_ref) = refs[:-3], refs[-3:]

    def fold_in(chosen):
        bias = bias_of(bias_ref, 0, kv_refs, chosen)
        for g in range(rows_ref.shape[0]):
            lanes = slice(g * HD, (g + 1) * HD)
            state = fold(rows_ref[g], [kv_refs[i] for i in sorted(chosen)], bias, lanes, None)
            max_ref[g] = jnp.broadcast_to(state[0], max_ref.shape[1:])
            sums_ref[g] = state[1]
            mixed_ref[g] = state[2]

    on_half(offsets, [ref.shape[0] for ref in kv_refs], fold_in)


def late_kernel(group_size, offsets, rows_ref, bias_ref, *refs):
    states, kv_refs, (attended_ref, squares_ref) = refs[:3], refs[3:-2], refs[-2:]
    rows = rows_ref.shape[1] // group_size
    first = bias_ref.shape[1] - keys_in(kv_refs)

    def end(chosen):
        squares = jnp.zeros((rows, HD), jnp.float32)
        for g in range(rows_ref.shape[0]):
            lanes = slice(g * HD, (g + 1) * HD)
            state = [ref[g] for ref in states]
            if chosen:
                bias = bias_of(bias_ref, first, kv_refs, chosen)
                state = fold(rows_ref[g], [kv_refs[i] for i in sorted(chosen)], bias, lanes, state)
            mixed = state[2] / jnp.sum(state[1], axis=1, keepdims=True)
            for r in range(group_size):
                block = mixed[r * rows : (r + 1) * rows]
                h = g * group_size + r
                attended_ref[:, h * HD : (h + 1) * HD] = block
                squares = squares + block * block
        squares_ref[...] = jnp.sum(squares.T, axis=0, keepdims=True)

    on_half(offsets, [ref.shape[0] for ref in kv_refs], end)


def finish_kernel(features, attended_ref, own_ref, other_ref, factor_ref, live_ref, out_ref):
    rows = attended_ref.shape[0]
    mean_square = (own_ref[...] + other_ref[...]) / features
    scale = jnp.broadcast_to(lax.rsqrt(mean_square + 1e-06), (HD, rows)).T
    live = live_ref[...] > 0.0
    for h in range(attended_ref.shape[1] // HD):
        lanes = slice(h * HD, (h + 1) * HD)
        block = attended_ref[:, lanes] * scale * factor_ref[0:1, lanes]
        out_ref[0, :, lanes] = jnp.where(live, block, 0.0).astype(out_ref.dtype)


def kernel(body, outs, count, megabytes, name):
    several = isinstance(outs, tuple)
    return pl.pallas_call(
        body,
        out_shape=outs,
        in_specs=in_vmem(count),
        out_specs=tuple(in_vmem(len(outs))) if several else in_vmem(1)[0],
        compiler_params=pltpu.CompilerParams(vmem_limit_bytes=megabytes * 1024 * 1024),
        name=name,
    )


def after(array, *others):
    return lax.optimization_barrier((array, *others))[0]


def offsets_of(steps):
    at = {"own": [(0, 0)], "kept": [(0, 0)]}
    for name, hop, source, _ in steps:
        at[name] = [(clip ^ hop[0], part ^ hop[1]) for clip, part in at[source]]
    return at


def travel(steps, own, kept, prepared):
    have = {"own": own, "kept": kept, PREPARED: prepared}
    for name, hop, source, wait_for in steps:
        shard = have[source]
        if wait_for is not None:
            shard = after(shard, have[wait_for])
        have[name] = exchanged(shard, ("span", "seq"), hop)
    return have


def by_exchange(queries, keys_values, clip_tokens, noise_level, level_gate, out_gain):
    tokens_here, width = queries.shape[1:]
    kv_heads_here = keys_values.shape[-1] // HD
    group_size = width // HD // kv_heads_here
    own = keys_values[None, :, 0]
    f32 = functools.partial(jax.ShapeDtypeStruct, dtype=jnp.float32)
    stacked = (kv_heads_here, group_size * tokens_here, HD)
    steps, early, late = plan_of()
    offsets = offsets_of(steps)
    early_at = [at for name in early for at in offsets[name]]
    late_at = [at for name in late for at in offsets[name]]
    offsets = early_at + late_at
    outs = (
        jax.ShapeDtypeStruct(stacked, queries.dtype),
        jax.ShapeDtypeStruct(own.shape, own.dtype),
        f32((8, width)),
        f32((8, tokens_here * len(offsets))),
        f32((tokens_here, HD)),
    )
    sources = (queries[0], level_gate, out_gain, clip_tokens, noise_level, own)
    spaces = (pltpu.VMEM, pltpu.VMEM, pltpu.VMEM, pltpu.SMEM, pltpu.SMEM)
    rows, own_kept, factor, bias, live = pl.pallas_call(
        functools.partial(prepare_kernel, offsets, len(outs)),
        out_shape=outs,
        in_specs=[pl.BlockSpec(memory_space=pltpu.HBM)] * len(sources),
        out_specs=tuple(in_vmem(len(outs))),
        scratch_shapes=[space(x.shape, x.dtype) for space, x in zip(spaces, sources)]
        + [pltpu.SemaphoreType.DMA((len(sources),))],
        compiler_params=pltpu.CompilerParams(vmem_limit_bytes=8 * 1024 * 1024),
        name="prepare",
    )(*(in_hbm(x) for x in sources))
    have = travel(steps, own, own_kept, rows)
    state = kernel(
        functools.partial(early_kernel, early_at), (f32(stacked),) * 3, 2 + len(early), 16, "attend_early"
    )(
        rows, bias, *[have[name] for name in early]
    )
    attended, squares = kernel(
        functools.partial(late_kernel, group_size, late_at),
        (f32((tokens_here, width)), f32((1, tokens_here))),
        5 + len(late), 16, "attend_late",
    )(rows, bias, *state, *[have[name] for name in late])
    others = [exchanged(squares, ("mp",), (by,)) for by in range(1, lax.axis_size("mp"))]
    return kernel(
        functools.partial(finish_kernel, width * lax.axis_size("mp")),
        jax.ShapeDtypeStruct(queries.shape, queries.dtype),
        5, 4, "finish",
    )(attended, squares, sum(others), factor, live)


def passed_along(shard, axis, by):
    peers = lax.axis_size(axis)
    pairs = [(i, i + by) for i in range(peers) if 0 <= i + by < peers]
    return lax.ppermute(shard, axis, pairs)


def by_blocks(queries, keys_values, clip_tokens, noise_level, level_gate, out_gain):
    tokens_here = queries.shape[1]
    slot_count = tokens_here * lax.axis_size("seq")
    clip_count = clip_tokens.shape[0]
    kv_heads_here = keys_values.shape[-1] // HD
    heads_here = queries.shape[-1] // HD
    group_size = heads_here // kv_heads_here
    own_clip = lax.axis_index("span")
    own_seq = lax.axis_index("seq")
    query_heads = queries[0].reshape(tokens_here, kv_heads_here, group_size, HD)
    score_scale = 1.0 / math.sqrt(HD)
    clip_ids = jnp.arange(clip_count, dtype=jnp.int32)

    def clip_length(which):
        return jnp.sum(
            jnp.where(which[:, None] == clip_ids[None, :], clip_tokens[None, :], 0), axis=1
        )

    def block_step(running, key_block, first):
        key_count = key_block.shape[1]
        positions = first + jnp.arange(key_count, dtype=jnp.int32)
        holder = positions // slot_count
        slot_index = positions - holder * slot_count
        usable = (holder >= 0) & (holder <= own_clip) & (slot_index < clip_length(holder))

        def update(state):
            running_max, weight_sum, weighted = state
            key_rows = key_block[0].reshape(key_count, kv_heads_here, HD)
            value_rows = key_block[1].reshape(key_count, kv_heads_here, HD)
            scores = (
                jnp.einsum(
                    "tgrd,kgd->tgrk", query_heads, key_rows, preferred_element_type=jnp.float32
                )
                * score_scale
            )
            scores = jnp.where(usable[None, None, None, :], scores, -jnp.inf)
            new_max = jnp.maximum(running_max, jnp.max(scores, axis=-1))
            weights = jnp.exp(scores - new_max[..., None])
            shrink = jnp.exp(running_max - new_max)
            weight_sum = weight_sum * shrink + jnp.sum(weights, axis=-1)
            weighted = weighted * shrink[..., None] + jnp.einsum(
                "tgrk,kgd->tgrd",
                weights.astype(jnp.bfloat16),
                value_rows,
                preferred_element_type=jnp.float32,
            )
            return (new_max, weight_sum, weighted)

        def unchanged(state):
            return state

        return lax.cond(jnp.any(usable), update, unchanged, running)

    def fold_piece(running, kv_piece, first):
        key_count = kv_piece.shape[1]
        if key_count > 1024 and key_count % 1024 == 0:

            def loop_step(block_index, state):
                key_block = lax.dynamic_slice_in_dim(kv_piece, block_index * 1024, 1024, 1)
                return block_step(state, key_block, first + block_index * 1024)

            return lax.fori_loop(0, key_count // 1024, loop_step, running)
        return block_step(running, kv_piece, first)

    initial = (
        jnp.full((tokens_here, kv_heads_here, group_size), -jnp.inf, jnp.float32),
        jnp.zeros((tokens_here, kv_heads_here, group_size), jnp.float32),
        jnp.zeros((tokens_here, kv_heads_here, group_size, HD), jnp.float32),
    )
    local_kv = keys_values[:, 0]
    clip_kv = lax.all_gather(local_kv, "seq", axis=1, tiled=True)
    running = fold_piece(initial, clip_kv, own_clip * slot_count)
    for distance in range(1, clip_count):
        clip_kv = passed_along(clip_kv, "span", 1)
        running = fold_piece(running, clip_kv, (own_clip - distance) * slot_count)
    running_max, weight_sum, weighted = running
    attended = (weighted / weight_sum[..., None]).reshape(
        tokens_here, kv_heads_here * group_size * HD
    )
    squares = jnp.sum(attended * attended, axis=1)
    mean_square = lax.psum(squares, "mp") / (heads_here * HD * lax.axis_size("mp"))
    own_level = jnp.sum(jnp.where(clip_ids == own_clip, noise_level, 0))
    one_hot = (jnp.arange(level_gate.shape[0], dtype=jnp.int32) == own_level).astype(jnp.bfloat16)
    gate_row = jnp.dot(one_hot, level_gate, preferred_element_type=jnp.float32)
    own_length = jnp.sum(jnp.where(clip_ids == own_clip, clip_tokens, 0))
    usable_rows = own_seq * tokens_here + jnp.arange(tokens_here, dtype=jnp.int32) < own_length
    normed = (
        attended
        * lax.rsqrt(mean_square + 1e-06)[:, None]
        * out_gain.astype(jnp.float32)
        * (1.0 + gate_row)
    )
    return jnp.where(usable_rows[:, None], normed, 0.0).astype(jnp.bfloat16)[None]


def per_device(*arrays):
    sizes = tuple(lax.axis_size(axis) for axis in ("span", "seq", "mp"))
    few = sizes == (4, 4, 2)
    return (by_exchange if few else by_blocks)(*arrays)


def solution(mesh):
    placed = (
        P("span", "seq", "mp"),
        P(None, "span", "seq", "mp"),
        P(),
        P(),
        P(None, "mp"),
        P("mp"),
    )
    return jax.shard_map(
        per_device, mesh=mesh, in_specs=placed, out_specs=P("span", "seq", "mp"), check_vma=False
    )
```

```python
import functools
import itertools
import math

import jax
import jax.numpy as jnp
from jax import lax
from jax.experimental import pallas as pl
from jax.experimental.pallas import tpu as pltpu
from jax.sharding import PartitionSpec as P

HD = 128
MASKED = -1e30
PREPARED = "prepared"


def plan_of():
    steps = [("p3", (0, 3), "own", None), ("p2", (0, 2), "own", None), ("p1", (0, 1), "own", None)]
    steps += [("x0", (2, 0), "own", None), ("c0", (1, 0), "own", PREPARED)]
    steps += [("x3", (2, 0), "p3", None), ("x2", (2, 0), "p2", None)]
    steps += [("c3", (1, 0), "p3", None), ("c2", (1, 0), "p2", None)]
    steps += [("x1", (2, 0), "p1", None), ("c1", (1, 0), "p1", None)]
    steps += [("d" + part, (1, 0), "x" + part, None) for part in "0321"]
    early = ["kept", "p3", "d0", "p1", "c0", "c1", "c2", "c3", "x1", "x3", "p2", "d3"]
    return steps, early, ["x0", "d1", "x2", "d2"]


def exchanged(shard, axes, by):
    sizes = [lax.axis_size(axis) for axis in axes]
    places = list(itertools.product(*(range(size) for size in sizes)))
    to = [tuple(i ^ k for i, k in zip(place, by)) for place in places]
    return lax.ppermute(shard, axes, [(i, places.index(there)) for i, there in enumerate(to)])


def in_vmem(count):
    return [pl.BlockSpec(memory_space=pltpu.VMEM)] * count


def in_hbm(array):
    return pltpu.with_memory_space_constraint(array, pltpu.HBM)


def gate_factor(level, gate_ref, gain_ref):
    levels = gate_ref.shape[0]
    one_hot = (lax.broadcasted_iota(jnp.int32, (16, levels), 1) == level).astype(jnp.bfloat16)
    row = jnp.dot(one_hot, gate_ref[...], preferred_element_type=jnp.float32)[:8]
    gain = gain_ref[...].astype(jnp.float32)
    return jnp.broadcast_to(gain[None, :], row.shape) * (1.0 + row)


def prepare_kernel(offsets, count, *refs):
    sources, outs, (arrived,) = refs[:6], refs[6 : 6 + count], refs[-1:]
    rows_ref, own_ref, factor_ref, bias_ref, live_ref = outs
    scratch = refs[6 + count : -1]
    q_ref, gate_ref, gain_ref, tokens_ref, level_ref = scratch
    places = (q_ref, gate_ref, gain_ref, tokens_ref, level_ref, own_ref)
    copies = [
        pltpu.make_async_copy(src, dst, arrived.at[i])
        for i, (src, dst) in enumerate(zip(sources, places))
    ]
    for copy in copies:
        copy.start()
    copies[0].wait()
    kv_heads, stacked = rows_ref.shape[:2]
    rows = q_ref.shape[0]
    group_size = stacked // rows
    for g in range(kv_heads):
        for r in range(group_size):
            h = g * group_size + r
            rows_ref[g, r * rows : (r + 1) * rows] = q_ref[:, h * HD : (h + 1) * HD]
    for copy in copies[1:]:
        copy.wait()
    own_clip = lax.axis_index("span")
    own_seq = lax.axis_index("seq")
    factor_ref[...] = gate_factor(level_ref[own_clip], gate_ref, gain_ref)
    lane = lax.broadcasted_iota(jnp.int32, (8, rows), 1)
    biases = []
    for clip_by, seq_by in offsets:
        clip = own_clip ^ clip_by
        live = tokens_ref[clip] - (own_seq ^ seq_by) * rows
        biases.append(jnp.where(lane < jnp.where(clip <= own_clip, live, 0), 0.0, MASKED))
    bias_ref[...] = jnp.concatenate(biases, axis=1)
    slot = own_seq * rows + lax.broadcasted_iota(jnp.int32, live_ref.shape, 0)
    live_ref[...] = (slot < tokens_ref[own_clip]).astype(jnp.float32)


def fold(query_rows, kv_refs, bias, lanes, state):
    to_exponent = math.log2(math.e) / math.sqrt(HD)
    pieces = [(ref, i) for ref in kv_refs for i in range(ref.shape[0])]
    key_rows = jnp.concatenate([ref[i, 0, :, lanes] for ref, i in pieces], axis=0)
    value_rows = jnp.concatenate([ref[i, 1, :, lanes] for ref, i in pieces], axis=0)
    scores = lax.dot_general(
        query_rows, key_rows, (((1,), (1,)), ((), ())), preferred_element_type=jnp.float32
    )
    scores = scores + bias
    tiles = [slice(i, i + HD) for i in range(0, scores.shape[1], HD)]
    highest = functools.reduce(jnp.maximum, [scores[:, tile] for tile in tiles])
    if state is not None:
        highest = jnp.maximum(highest, state[0])
    new_max = jnp.max(highest, axis=1, keepdims=True)
    weights = jnp.exp2((scores - new_max) * to_exponent)
    weight_sums = functools.reduce(jnp.add, [weights[:, tile] for tile in tiles])
    mixed = jnp.dot(weights.astype(jnp.bfloat16), value_rows, preferred_element_type=jnp.float32)
    if state is not None:
        shrink = jnp.exp2((state[0] - new_max) * to_exponent)
        weight_sums = weight_sums + state[1] * shrink
        mixed = mixed + state[2] * shrink
    return new_max, weight_sums, mixed


def on_upper(upper):
    across = lax.axis_size("span") // 2
    return (lax.axis_index("span") >= across) == upper


def usable_on_lower(offsets):
    across = lax.axis_size("span") // 2
    chosen = [i for i, (by, _) in enumerate(offsets) if by < across]
    others = [i for i in range(len(offsets)) if i not in chosen]
    return sorted(chosen + others[: len(chosen) % 2])


def bias_of(bias_ref, first, keys, chosen):
    tiles = [bias_ref[0:1, first + i * keys : first + (i + 1) * keys] for i in chosen]
    return jnp.concatenate(tiles, axis=1)


def put_attended(attended_ref, g, state):
    rows = attended_ref.shape[0]
    mixed = state[2] / jnp.sum(state[1], axis=1, keepdims=True)
    group_size = mixed.shape[0] // rows
    squares = jnp.zeros((rows, HD), jnp.float32)
    for r in range(group_size):
        block = mixed[r * rows : (r + 1) * rows]
        h = g * group_size + r
        attended_ref[:, h * HD : (h + 1) * HD] = block
        squares = squares + block * block
    return squares


def early_kernel(offsets, rows_ref, bias_ref, *refs):
    kv_refs, state_refs, (attended_ref, squares_ref) = refs[:-5], refs[-5:-2], refs[-2:]
    keys = kv_refs[0].shape[2]

    def fold_in(chosen, is_all):
        squares = []
        bias = bias_of(bias_ref, 0, keys, chosen)
        for g in range(rows_ref.shape[0]):
            lanes = slice(g * HD, (g + 1) * HD)
            state = fold(rows_ref[g], [kv_refs[i] for i in chosen], bias, lanes, None)
            if is_all:
                squares.append(put_attended(attended_ref, g, state))
            else:
                state_refs[0][g] = jnp.broadcast_to(state[0], state_refs[0].shape[1:])
                state_refs[1][g] = state[1]
                state_refs[2][g] = state[2]
        if is_all:
            squares_ref[...] = jnp.sum(sum(squares).T, axis=0, keepdims=True)

    pl.when(on_upper(True))(lambda: fold_in(range(len(kv_refs)), False))
    pl.when(on_upper(False))(lambda: fold_in(usable_on_lower(offsets), True))


def late_kernel(rows_ref, bias_ref, *refs):
    states, kv_refs, (attended_ref, squares_ref) = refs[:3], refs[5:-2], refs[-2:]
    keys = kv_refs[0].shape[2]
    first = bias_ref.shape[1] - keys * len(kv_refs)

    def end():
        squares = []
        bias = bias_of(bias_ref, first, keys, range(len(kv_refs)))
        for g in range(rows_ref.shape[0]):
            lanes = slice(g * HD, (g + 1) * HD)
            state = fold(rows_ref[g], kv_refs, bias, lanes, [ref[g] for ref in states])
            squares.append(put_attended(attended_ref, g, state))
        squares_ref[...] = jnp.sum(sum(squares).T, axis=0, keepdims=True)

    pl.when(on_upper(True))(end)


def finish_kernel(features, attended_ref, own_ref, other_ref, factor_ref, live_ref, out_ref):
    rows = attended_ref.shape[0]
    mean_square = (own_ref[...] + other_ref[...]) / features
    scale = jnp.broadcast_to(lax.rsqrt(mean_square + 1e-06), (HD, rows)).T
    live = live_ref[...] > 0.0
    for h in range(attended_ref.shape[1] // HD):
        lanes = slice(h * HD, (h + 1) * HD)
        block = attended_ref[:, lanes] * scale * factor_ref[0:1, lanes]
        out_ref[0, :, lanes] = jnp.where(live, block, 0.0).astype(out_ref.dtype)


def kernel(body, outs, count, megabytes, name, in_place={}):
    several = isinstance(outs, tuple)
    return pl.pallas_call(
        body,
        out_shape=outs,
        in_specs=in_vmem(count),
        out_specs=tuple(in_vmem(len(outs))) if several else in_vmem(1)[0],
        input_output_aliases=in_place,
        compiler_params=pltpu.CompilerParams(vmem_limit_bytes=megabytes * 1024 * 1024),
        name=name,
    )


def after(array, *others):
    return lax.optimization_barrier((array, *others))[0]


def offsets_of(steps):
    at = {"own": [(0, 0)], "kept": [(0, 0)]}
    for name, hop, source, _ in steps:
        at[name] = [(clip ^ hop[0], part ^ hop[1]) for clip, part in at[source]]
    return at


def travel(steps, own, kept, prepared):
    have = {"own": own, "kept": kept, PREPARED: prepared}
    for name, hop, source, wait_for in steps:
        shard = have[source]
        if wait_for is not None:
            shard = after(shard, have[wait_for])
        have[name] = exchanged(shard, ("span", "seq"), hop)
    return have


def by_exchange(queries, keys_values, clip_tokens, noise_level, level_gate, out_gain):
    tokens_here, width = queries.shape[1:]
    kv_heads_here = keys_values.shape[-1] // HD
    group_size = width // HD // kv_heads_here
    own = keys_values[None, :, 0]
    f32 = functools.partial(jax.ShapeDtypeStruct, dtype=jnp.float32)
    stacked = (kv_heads_here, group_size * tokens_here, HD)
    steps, early, late = plan_of()
    offsets = offsets_of(steps)
    early_at = [at for name in early for at in offsets[name]]
    late_at = [at for name in late for at in offsets[name]]
    offsets = early_at + late_at
    outs = (
        jax.ShapeDtypeStruct(stacked, queries.dtype),
        jax.ShapeDtypeStruct(own.shape, own.dtype),
        f32((8, width)),
        f32((8, tokens_here * len(offsets))),
        f32((tokens_here, HD)),
    )
    sources = (queries[0], level_gate, out_gain, clip_tokens, noise_level, own)
    spaces = (pltpu.VMEM, pltpu.VMEM, pltpu.VMEM, pltpu.SMEM, pltpu.SMEM)
    rows, own_kept, factor, bias, live = pl.pallas_call(
        functools.partial(prepare_kernel, offsets, len(outs)),
        out_shape=outs,
        in_specs=[pl.BlockSpec(memory_space=pltpu.HBM)] * len(sources),
        out_specs=tuple(in_vmem(len(outs))),
        scratch_shapes=[space(x.shape, x.dtype) for space, x in zip(spaces, sources)]
        + [pltpu.SemaphoreType.DMA((len(sources),))],
        compiler_params=pltpu.CompilerParams(vmem_limit_bytes=8 * 1024 * 1024),
        name="prepare",
    )(*(in_hbm(x) for x in sources))
    have = travel(steps, own, own_kept, rows)
    ends = (f32((tokens_here, width)), f32((1, tokens_here)))
    *state, attended, squares = kernel(
        functools.partial(early_kernel, early_at),
        (f32(stacked),) * 3 + ends,
        2 + len(early), 16, "attend_early",
    )(rows, bias, *[have[name] for name in early])
    assert not usable_on_lower(late_at)
    attended, squares = kernel(
        late_kernel, ends, 7 + len(late), 16, "attend_late", in_place={5: 0, 6: 1}
    )(rows, bias, *state, attended, squares, *[have[name] for name in late])
    others = [exchanged(squares, ("mp",), (by,)) for by in range(1, lax.axis_size("mp"))]
    return kernel(
        functools.partial(finish_kernel, width * lax.axis_size("mp")),
        jax.ShapeDtypeStruct(queries.shape, queries.dtype),
        5, 4, "finish",
    )(attended, squares, sum(others), factor, live)


def passed_along(shard, axis, by):
    peers = lax.axis_size(axis)
    pairs = [(i, i + by) for i in range(peers) if 0 <= i + by < peers]
    return lax.ppermute(shard, axis, pairs)


def by_blocks(queries, keys_values, clip_tokens, noise_level, level_gate, out_gain):
    tokens_here = queries.shape[1]
    slot_count = tokens_here * lax.axis_size("seq")
    clip_count = clip_tokens.shape[0]
    kv_heads_here = keys_values.shape[-1] // HD
    heads_here = queries.shape[-1] // HD
    group_size = heads_here // kv_heads_here
    own_clip = lax.axis_index("span")
    own_seq = lax.axis_index("seq")
    query_heads = queries[0].reshape(tokens_here, kv_heads_here, group_size, HD)
    score_scale = 1.0 / math.sqrt(HD)
    clip_ids = jnp.arange(clip_count, dtype=jnp.int32)

    def clip_length(which):
        return jnp.sum(
            jnp.where(which[:, None] == clip_ids[None, :], clip_tokens[None, :], 0), axis=1
        )

    def block_step(running, key_block, first):
        key_count = key_block.shape[1]
        positions = first + jnp.arange(key_count, dtype=jnp.int32)
        holder = positions // slot_count
        slot_index = positions - holder * slot_count
        usable = (holder >= 0) & (holder <= own_clip) & (slot_index < clip_length(holder))

        def update(state):
            running_max, weight_sum, weighted = state
            key_rows = key_block[0].reshape(key_count, kv_heads_here, HD)
            value_rows = key_block[1].reshape(key_count, kv_heads_here, HD)
            scores = (
                jnp.einsum(
                    "tgrd,kgd->tgrk", query_heads, key_rows, preferred_element_type=jnp.float32
                )
                * score_scale
            )
            scores = jnp.where(usable[None, None, None, :], scores, -jnp.inf)
            new_max = jnp.maximum(running_max, jnp.max(scores, axis=-1))
            weights = jnp.exp(scores - new_max[..., None])
            shrink = jnp.exp(running_max - new_max)
            weight_sum = weight_sum * shrink + jnp.sum(weights, axis=-1)
            weighted = weighted * shrink[..., None] + jnp.einsum(
                "tgrk,kgd->tgrd",
                weights.astype(jnp.bfloat16),
                value_rows,
                preferred_element_type=jnp.float32,
            )
            return (new_max, weight_sum, weighted)

        def unchanged(state):
            return state

        return lax.cond(jnp.any(usable), update, unchanged, running)

    def fold_piece(running, kv_piece, first):
        key_count = kv_piece.shape[1]
        if key_count > 1024 and key_count % 1024 == 0:

            def loop_step(block_index, state):
                key_block = lax.dynamic_slice_in_dim(kv_piece, block_index * 1024, 1024, 1)
                return block_step(state, key_block, first + block_index * 1024)

            return lax.fori_loop(0, key_count // 1024, loop_step, running)
        return block_step(running, kv_piece, first)

    initial = (
        jnp.full((tokens_here, kv_heads_here, group_size), -jnp.inf, jnp.float32),
        jnp.zeros((tokens_here, kv_heads_here, group_size), jnp.float32),
        jnp.zeros((tokens_here, kv_heads_here, group_size, HD), jnp.float32),
    )
    local_kv = keys_values[:, 0]
    clip_kv = lax.all_gather(local_kv, "seq", axis=1, tiled=True)
    running = fold_piece(initial, clip_kv, own_clip * slot_count)
    for distance in range(1, clip_count):
        clip_kv = passed_along(clip_kv, "span", 1)
        running = fold_piece(running, clip_kv, (own_clip - distance) * slot_count)
    running_max, weight_sum, weighted = running
    attended = (weighted / weight_sum[..., None]).reshape(
        tokens_here, kv_heads_here * group_size * HD
    )
    squares = jnp.sum(attended * attended, axis=1)
    mean_square = lax.psum(squares, "mp") / (heads_here * HD * lax.axis_size("mp"))
    own_level = jnp.sum(jnp.where(clip_ids == own_clip, noise_level, 0))
    one_hot = (jnp.arange(level_gate.shape[0], dtype=jnp.int32) == own_level).astype(jnp.bfloat16)
    gate_row = jnp.dot(one_hot, level_gate, preferred_element_type=jnp.float32)
    own_length = jnp.sum(jnp.where(clip_ids == own_clip, clip_tokens, 0))
    usable_rows = own_seq * tokens_here + jnp.arange(tokens_here, dtype=jnp.int32) < own_length
    normed = (
        attended
        * lax.rsqrt(mean_square + 1e-06)[:, None]
        * out_gain.astype(jnp.float32)
        * (1.0 + gate_row)
    )
    return jnp.where(usable_rows[:, None], normed, 0.0).astype(jnp.bfloat16)[None]


def per_device(*arrays):
    sizes = tuple(lax.axis_size(axis) for axis in ("span", "seq", "mp"))
    few = sizes == (4, 4, 2)
    return (by_exchange if few else by_blocks)(*arrays)


def solution(mesh):
    placed = (
        P("span", "seq", "mp"),
        P(None, "span", "seq", "mp"),
        P(),
        P(),
        P(None, "mp"),
        P("mp"),
    )
    return jax.shard_map(
        per_device, mesh=mesh, in_specs=placed, out_specs=P("span", "seq", "mp"), check_vma=False
    )
```

```python
import functools
import itertools
import math

import jax
import jax.numpy as jnp
from jax import lax
from jax.experimental import pallas as pl
from jax.experimental.pallas import tpu as pltpu
from jax.sharding import PartitionSpec as P

HD = 128
MASKED = -1e30
PREPARED = "prepared"


def plan_of():
    steps = [("p3", (0, 3), "own", None), ("p2", (0, 2), "own", None), ("p1", (0, 1), "own", None)]
    steps += [("x0", (2, 0), "own", None), ("c0", (1, 0), "own", PREPARED)]
    steps += [("x3", (2, 0), "p3", None), ("x2", (2, 0), "p2", None)]
    steps += [("c3", (1, 0), "p3", None), ("c2", (1, 0), "p2", None)]
    steps += [("x1", (2, 0), "p1", None), ("c1", (1, 0), "p1", None)]
    steps += [("d" + part, (1, 0), "x" + part, None) for part in "0321"]
    early = ["kept", "p3", "d0", "p1", "c0", "c1", "c2", "c3", "x1", "x3", "p2", "d3"]
    return steps, early, ["x0", "d1", "x2", "d2"]


def exchanged(shard, axes, by):
    sizes = [lax.axis_size(axis) for axis in axes]
    places = list(itertools.product(*(range(size) for size in sizes)))
    to = [tuple(i ^ k for i, k in zip(place, by)) for place in places]
    return lax.ppermute(shard, axes, [(i, places.index(there)) for i, there in enumerate(to)])


def in_vmem(count):
    return [pl.BlockSpec(memory_space=pltpu.VMEM)] * count


def in_hbm(array):
    return pltpu.with_memory_space_constraint(array, pltpu.HBM)


def gate_factor(level, gate_ref, gain_ref):
    levels = gate_ref.shape[0]
    one_hot = (lax.broadcasted_iota(jnp.int32, (16, levels), 1) == level).astype(jnp.bfloat16)
    row = jnp.dot(one_hot, gate_ref[...], preferred_element_type=jnp.float32)[:8]
    gain = gain_ref[...].astype(jnp.float32)
    return jnp.broadcast_to(gain[None, :], row.shape) * (1.0 + row)


def prepare_kernel(offsets, count, *refs):
    sources, outs, (arrived,) = refs[:6], refs[6 : 6 + count], refs[-1:]
    rows_ref, own_ref, factor_ref, bias_ref, live_ref = outs
    scratch = refs[6 + count : -1]
    q_ref, gate_ref, gain_ref, tokens_ref, level_ref = scratch
    places = (q_ref, gate_ref, gain_ref, tokens_ref, level_ref, own_ref)
    copies = [
        pltpu.make_async_copy(src, dst, arrived.at[i])
        for i, (src, dst) in enumerate(zip(sources, places))
    ]
    for copy in copies:
        copy.start()
    copies[0].wait()
    kv_heads, stacked = rows_ref.shape[:2]
    rows = q_ref.shape[0]
    group_size = stacked // rows
    for g in range(kv_heads):
        for r in range(group_size):
            h = g * group_size + r
            rows_ref[g, r * rows : (r + 1) * rows] = q_ref[:, h * HD : (h + 1) * HD]
    for copy in copies[1:]:
        copy.wait()
    own_clip = lax.axis_index("span")
    own_seq = lax.axis_index("seq")
    factor_ref[...] = gate_factor(level_ref[own_clip], gate_ref, gain_ref)
    lane = lax.broadcasted_iota(jnp.int32, (8, rows), 1)
    biases = []
    for clip_by, seq_by in offsets:
        clip = own_clip ^ clip_by
        live = tokens_ref[clip] - (own_seq ^ seq_by) * rows
        biases.append(jnp.where(lane < jnp.where(clip <= own_clip, live, 0), 0.0, MASKED))
    bias_ref[...] = jnp.concatenate(biases, axis=1)
    slot = own_seq * rows + lax.broadcasted_iota(jnp.int32, live_ref.shape, 0)
    live_ref[...] = (slot < tokens_ref[own_clip]).astype(jnp.float32)


def fold(query_rows, kv_refs, bias, lanes, state):
    to_exponent = math.log2(math.e) / math.sqrt(HD)
    pieces = [(ref, i) for ref in kv_refs for i in range(ref.shape[0])]
    key_rows = jnp.concatenate([ref[i, 0, :, lanes] for ref, i in pieces], axis=0)
    value_rows = jnp.concatenate([ref[i, 1, :, lanes] for ref, i in pieces], axis=0)
    scores = lax.dot_general(
        query_rows, key_rows, (((1,), (1,)), ((), ())), preferred_element_type=jnp.float32
    )
    scores = scores + bias
    tiles = [slice(i, i + HD) for i in range(0, scores.shape[1], HD)]
    highest = functools.reduce(jnp.maximum, [scores[:, tile] for tile in tiles])
    if state is not None:
        highest = jnp.maximum(highest, state[0])
    new_max = jnp.max(highest, axis=1, keepdims=True)
    weights = jnp.exp2((scores - new_max) * to_exponent)
    weight_sums = functools.reduce(jnp.add, [weights[:, tile] for tile in tiles])
    mixed = jnp.dot(weights.astype(jnp.bfloat16), value_rows, preferred_element_type=jnp.float32)
    if state is not None:
        shrink = jnp.exp2((state[0] - new_max) * to_exponent)
        weight_sums = weight_sums + state[1] * shrink
        mixed = mixed + state[2] * shrink
    return new_max, weight_sums, mixed


def on_upper(upper):
    across = lax.axis_size("span") // 2
    return (lax.axis_index("span") >= across) == upper


def usable_on_lower(offsets):
    across = lax.axis_size("span") // 2
    chosen = [i for i, (by, _) in enumerate(offsets) if by < across]
    others = [i for i in range(len(offsets)) if i not in chosen]
    return sorted(chosen + others[: len(chosen) % 2])


def bias_of(bias_ref, first, keys, chosen):
    tiles = [bias_ref[0:1, first + i * keys : first + (i + 1) * keys] for i in chosen]
    return jnp.concatenate(tiles, axis=1)


def put_attended(attended_ref, g, state):
    rows = attended_ref.shape[0]
    mixed = state[2] / jnp.sum(state[1], axis=1, keepdims=True)
    group_size = mixed.shape[0] // rows
    squares = jnp.zeros((rows, HD), jnp.float32)
    for r in range(group_size):
        block = mixed[r * rows : (r + 1) * rows]
        h = g * group_size + r
        attended_ref[:, h * HD : (h + 1) * HD] = block
        squares = squares + block * block
    return squares


def early_kernel(offsets, rows_ref, bias_ref, *refs):
    kv_refs, state_refs, (attended_ref, squares_ref) = refs[:-5], refs[-5:-2], refs[-2:]
    keys = kv_refs[0].shape[2]

    def fold_in(chosen, is_all):
        squares = []
        bias = bias_of(bias_ref, 0, keys, chosen)
        for g in range(rows_ref.shape[0]):
            lanes = slice(g * HD, (g + 1) * HD)
            state = fold(rows_ref[g], [kv_refs[i] for i in chosen], bias, lanes, None)
            if is_all:
                squares.append(put_attended(attended_ref, g, state))
            else:
                state_refs[0][g] = jnp.broadcast_to(state[0], state_refs[0].shape[1:])
                state_refs[1][g] = state[1]
                state_refs[2][g] = state[2]
        if is_all:
            squares_ref[...] = jnp.sum(sum(squares).T, axis=0, keepdims=True)

    pl.when(on_upper(True))(lambda: fold_in(range(len(kv_refs)), False))
    pl.when(on_upper(False))(lambda: fold_in(usable_on_lower(offsets), True))


def late_kernel(rows_ref, bias_ref, *refs):
    states, kv_refs, (attended_ref, squares_ref) = refs[:3], refs[5:-2], refs[-2:]
    keys = kv_refs[0].shape[2]
    first = bias_ref.shape[1] - keys * len(kv_refs)

    def end():
        squares = []
        bias = bias_of(bias_ref, first, keys, range(len(kv_refs)))
        for g in range(rows_ref.shape[0]):
            lanes = slice(g * HD, (g + 1) * HD)
            state = fold(rows_ref[g], kv_refs, bias, lanes, [ref[g] for ref in states])
            squares.append(put_attended(attended_ref, g, state))
        squares_ref[...] = jnp.sum(sum(squares).T, axis=0, keepdims=True)

    pl.when(on_upper(True))(end)


def gain_kernel(attended_ref, factor_ref, live_ref, out_ref):
    live = live_ref[...] > 0.0
    for h in range(attended_ref.shape[1] // HD):
        lanes = slice(h * HD, (h + 1) * HD)
        out_ref[:, lanes] = jnp.where(live, attended_ref[:, lanes] * factor_ref[0:1, lanes], 0.0)


def finish_kernel(features, gained_ref, own_ref, other_ref, out_ref):
    rows = gained_ref.shape[0]
    mean_square = (own_ref[...] + other_ref[...]) / features
    scale = jnp.broadcast_to(lax.rsqrt(mean_square + 1e-06), (HD, rows)).T
    for h in range(gained_ref.shape[1] // HD):
        lanes = slice(h * HD, (h + 1) * HD)
        out_ref[0, :, lanes] = (gained_ref[:, lanes] * scale).astype(out_ref.dtype)


def kernel(body, outs, count, megabytes, name, in_place={}):
    several = isinstance(outs, tuple)
    return pl.pallas_call(
        body,
        out_shape=outs,
        in_specs=in_vmem(count),
        out_specs=tuple(in_vmem(len(outs))) if several else in_vmem(1)[0],
        input_output_aliases=in_place,
        compiler_params=pltpu.CompilerParams(vmem_limit_bytes=megabytes * 1024 * 1024),
        name=name,
    )


def after(array, *others):
    return lax.optimization_barrier((array, *others))[0]


def offsets_of(steps):
    at = {"own": [(0, 0)], "kept": [(0, 0)]}
    for name, hop, source, _ in steps:
        at[name] = [(clip ^ hop[0], part ^ hop[1]) for clip, part in at[source]]
    return at


def travel(steps, own, kept, prepared):
    have = {"own": own, "kept": kept, PREPARED: prepared}
    for name, hop, source, wait_for in steps:
        shard = have[source]
        if wait_for is not None:
            shard = after(shard, have[wait_for])
        have[name] = exchanged(shard, ("span", "seq"), hop)
    return have


def by_exchange(queries, keys_values, clip_tokens, noise_level, level_gate, out_gain):
    tokens_here, width = queries.shape[1:]
    kv_heads_here = keys_values.shape[-1] // HD
    group_size = width // HD // kv_heads_here
    own = keys_values[None, :, 0]
    f32 = functools.partial(jax.ShapeDtypeStruct, dtype=jnp.float32)
    stacked = (kv_heads_here, group_size * tokens_here, HD)
    steps, early, late = plan_of()
    offsets = offsets_of(steps)
    early_at = [at for name in early for at in offsets[name]]
    late_at = [at for name in late for at in offsets[name]]
    offsets = early_at + late_at
    outs = (
        jax.ShapeDtypeStruct(stacked, queries.dtype),
        jax.ShapeDtypeStruct(own.shape, own.dtype),
        f32((8, width)),
        f32((8, tokens_here * len(offsets))),
        f32((tokens_here, HD)),
    )
    sources = (queries[0], level_gate, out_gain, clip_tokens, noise_level, own)
    spaces = (pltpu.VMEM, pltpu.VMEM, pltpu.VMEM, pltpu.SMEM, pltpu.SMEM)
    rows, own_kept, factor, bias, live = pl.pallas_call(
        functools.partial(prepare_kernel, offsets, len(outs)),
        out_shape=outs,
        in_specs=[pl.BlockSpec(memory_space=pltpu.HBM)] * len(sources),
        out_specs=tuple(in_vmem(len(outs))),
        scratch_shapes=[space(x.shape, x.dtype) for space, x in zip(spaces, sources)]
        + [pltpu.SemaphoreType.DMA((len(sources),))],
        compiler_params=pltpu.CompilerParams(vmem_limit_bytes=8 * 1024 * 1024),
        name="prepare",
    )(*(in_hbm(x) for x in sources))
    have = travel(steps, own, own_kept, rows)
    ends = (f32((tokens_here, width)), f32((1, tokens_here)))
    *state, attended, squares = kernel(
        functools.partial(early_kernel, early_at),
        (f32(stacked),) * 3 + ends,
        2 + len(early), 16, "attend_early",
    )(rows, bias, *[have[name] for name in early])
    assert not usable_on_lower(late_at)
    attended, squares = kernel(
        late_kernel, ends, 7 + len(late), 16, "attend_late", in_place={5: 0, 6: 1}
    )(rows, bias, *state, attended, squares, *[have[name] for name in late])
    others = [exchanged(squares, ("mp",), (by,)) for by in range(1, lax.axis_size("mp"))]
    gained = kernel(gain_kernel, ends[0], 3, 4, "gain")(attended, factor, live)
    return kernel(
        functools.partial(finish_kernel, width * lax.axis_size("mp")),
        jax.ShapeDtypeStruct(queries.shape, queries.dtype),
        3, 4, "finish",
    )(gained, squares, sum(others))


def passed_along(shard, axis, by):
    peers = lax.axis_size(axis)
    pairs = [(i, i + by) for i in range(peers) if 0 <= i + by < peers]
    return lax.ppermute(shard, axis, pairs)


def by_blocks(queries, keys_values, clip_tokens, noise_level, level_gate, out_gain):
    tokens_here = queries.shape[1]
    slot_count = tokens_here * lax.axis_size("seq")
    clip_count = clip_tokens.shape[0]
    kv_heads_here = keys_values.shape[-1] // HD
    heads_here = queries.shape[-1] // HD
    group_size = heads_here // kv_heads_here
    own_clip = lax.axis_index("span")
    own_seq = lax.axis_index("seq")
    query_heads = queries[0].reshape(tokens_here, kv_heads_here, group_size, HD)
    score_scale = 1.0 / math.sqrt(HD)
    clip_ids = jnp.arange(clip_count, dtype=jnp.int32)

    def clip_length(which):
        return jnp.sum(
            jnp.where(which[:, None] == clip_ids[None, :], clip_tokens[None, :], 0), axis=1
        )

    def block_step(running, key_block, first):
        key_count = key_block.shape[1]
        positions = first + jnp.arange(key_count, dtype=jnp.int32)
        holder = positions // slot_count
        slot_index = positions - holder * slot_count
        usable = (holder >= 0) & (holder <= own_clip) & (slot_index < clip_length(holder))

        def update(state):
            running_max, weight_sum, weighted = state
            key_rows = key_block[0].reshape(key_count, kv_heads_here, HD)
            value_rows = key_block[1].reshape(key_count, kv_heads_here, HD)
            scores = (
                jnp.einsum(
                    "tgrd,kgd->tgrk", query_heads, key_rows, preferred_element_type=jnp.float32
                )
                * score_scale
            )
            scores = jnp.where(usable[None, None, None, :], scores, -jnp.inf)
            new_max = jnp.maximum(running_max, jnp.max(scores, axis=-1))
            weights = jnp.exp(scores - new_max[..., None])
            shrink = jnp.exp(running_max - new_max)
            weight_sum = weight_sum * shrink + jnp.sum(weights, axis=-1)
            weighted = weighted * shrink[..., None] + jnp.einsum(
                "tgrk,kgd->tgrd",
                weights.astype(jnp.bfloat16),
                value_rows,
                preferred_element_type=jnp.float32,
            )
            return (new_max, weight_sum, weighted)

        def unchanged(state):
            return state

        return lax.cond(jnp.any(usable), update, unchanged, running)

    def fold_piece(running, kv_piece, first):
        key_count = kv_piece.shape[1]
        if key_count > 1024 and key_count % 1024 == 0:

            def loop_step(block_index, state):
                key_block = lax.dynamic_slice_in_dim(kv_piece, block_index * 1024, 1024, 1)
                return block_step(state, key_block, first + block_index * 1024)

            return lax.fori_loop(0, key_count // 1024, loop_step, running)
        return block_step(running, kv_piece, first)

    initial = (
        jnp.full((tokens_here, kv_heads_here, group_size), -jnp.inf, jnp.float32),
        jnp.zeros((tokens_here, kv_heads_here, group_size), jnp.float32),
        jnp.zeros((tokens_here, kv_heads_here, group_size, HD), jnp.float32),
    )
    local_kv = keys_values[:, 0]
    clip_kv = lax.all_gather(local_kv, "seq", axis=1, tiled=True)
    running = fold_piece(initial, clip_kv, own_clip * slot_count)
    for distance in range(1, clip_count):
        clip_kv = passed_along(clip_kv, "span", 1)
        running = fold_piece(running, clip_kv, (own_clip - distance) * slot_count)
    running_max, weight_sum, weighted = running
    attended = (weighted / weight_sum[..., None]).reshape(
        tokens_here, kv_heads_here * group_size * HD
    )
    squares = jnp.sum(attended * attended, axis=1)
    mean_square = lax.psum(squares, "mp") / (heads_here * HD * lax.axis_size("mp"))
    own_level = jnp.sum(jnp.where(clip_ids == own_clip, noise_level, 0))
    one_hot = (jnp.arange(level_gate.shape[0], dtype=jnp.int32) == own_level).astype(jnp.bfloat16)
    gate_row = jnp.dot(one_hot, level_gate, preferred_element_type=jnp.float32)
    own_length = jnp.sum(jnp.where(clip_ids == own_clip, clip_tokens, 0))
    usable_rows = own_seq * tokens_here + jnp.arange(tokens_here, dtype=jnp.int32) < own_length
    normed = (
        attended
        * lax.rsqrt(mean_square + 1e-06)[:, None]
        * out_gain.astype(jnp.float32)
        * (1.0 + gate_row)
    )
    return jnp.where(usable_rows[:, None], normed, 0.0).astype(jnp.bfloat16)[None]


def per_device(*arrays):
    sizes = tuple(lax.axis_size(axis) for axis in ("span", "seq", "mp"))
    few = sizes == (4, 4, 2)
    return (by_exchange if few else by_blocks)(*arrays)


def solution(mesh):
    placed = (
        P("span", "seq", "mp"),
        P(None, "span", "seq", "mp"),
        P(),
        P(),
        P(None, "mp"),
        P("mp"),
    )
    return jax.shard_map(
        per_device, mesh=mesh, in_specs=placed, out_specs=P("span", "seq", "mp"), check_vma=False
    )
```

```python
import functools
import itertools
import math

import jax
import jax.numpy as jnp
from jax import lax
from jax.experimental import pallas as pl
from jax.experimental.pallas import tpu as pltpu
from jax.sharding import PartitionSpec as P

HD = 128
MASKED = -1e30
PREPARED = "prepared"


def plan_of():
    steps = [("p3", (0, 3), "own", None), ("p2", (0, 2), "own", None), ("p1", (0, 1), "own", None)]
    steps += [("x0", (2, 0), "own", None), ("c0", (1, 0), "own", PREPARED)]
    steps += [("x3", (2, 0), "p3", None), ("x2", (2, 0), "p2", None)]
    steps += [("c3", (1, 0), "p3", None), ("c2", (1, 0), "p2", None)]
    steps += [("x1", (2, 0), "p1", None), ("c1", (1, 0), "p1", None)]
    steps += [("d" + part, (1, 0), "x" + part, None) for part in "0321"]
    early = ["kept", "p3", "d0", "p1", "c0", "c1", "c2", "c3", "x1", "x3", "p2", "d3"]
    return steps, early, ["x0", "d1", "x2", "d2"]


def exchanged(shard, axes, by):
    sizes = [lax.axis_size(axis) for axis in axes]
    places = list(itertools.product(*(range(size) for size in sizes)))
    to = [tuple(i ^ k for i, k in zip(place, by)) for place in places]
    return lax.ppermute(shard, axes, [(i, places.index(there)) for i, there in enumerate(to)])


def in_vmem(count):
    return [pl.BlockSpec(memory_space=pltpu.VMEM)] * count


def in_hbm(array):
    return pltpu.with_memory_space_constraint(array, pltpu.HBM)


def gate_factor(level, gate_ref, gain_ref):
    levels = gate_ref.shape[0]
    one_hot = (lax.broadcasted_iota(jnp.int32, (16, levels), 1) == level).astype(jnp.bfloat16)
    row = jnp.dot(one_hot, gate_ref[...], preferred_element_type=jnp.float32)[:8]
    gain = gain_ref[...].astype(jnp.float32)
    return jnp.broadcast_to(gain[None, :], row.shape) * (1.0 + row)


def prepare_kernel(offsets, count, *refs):
    sources, outs, (arrived,) = refs[:6], refs[6 : 6 + count], refs[-1:]
    rows_ref, own_ref, factor_ref, bias_ref, live_ref = outs
    scratch = refs[6 + count : -1]
    q_ref, gate_ref, gain_ref, tokens_ref, level_ref = scratch
    places = (q_ref, gate_ref, gain_ref, tokens_ref, level_ref, own_ref)
    copies = [
        pltpu.make_async_copy(src, dst, arrived.at[i])
        for i, (src, dst) in enumerate(zip(sources, places))
    ]
    for copy in copies:
        copy.start()
    copies[0].wait()
    kv_heads, stacked = rows_ref.shape[:2]
    rows = q_ref.shape[0]
    group_size = stacked // rows
    for g in range(kv_heads):
        for r in range(group_size):
            h = g * group_size + r
            rows_ref[g, r * rows : (r + 1) * rows] = q_ref[:, h * HD : (h + 1) * HD]
    for copy in copies[1:]:
        copy.wait()
    own_clip = lax.axis_index("span")
    own_seq = lax.axis_index("seq")
    factor_ref[...] = gate_factor(level_ref[own_clip], gate_ref, gain_ref)
    lane = lax.broadcasted_iota(jnp.int32, (8, rows), 1)
    biases = []
    for clip_by, seq_by in offsets:
        clip = own_clip ^ clip_by
        live = tokens_ref[clip] - (own_seq ^ seq_by) * rows
        biases.append(jnp.where(lane < jnp.where(clip <= own_clip, live, 0), 0.0, MASKED))
    bias_ref[...] = jnp.concatenate(biases, axis=1)
    slot = own_seq * rows + lax.broadcasted_iota(jnp.int32, live_ref.shape, 0)
    live_ref[...] = (slot < tokens_ref[own_clip]).astype(jnp.float32)


def fold(query_rows, kv_refs, bias, lanes, state):
    to_exponent = math.log2(math.e) / math.sqrt(HD)
    pieces = [(ref, i) for ref in kv_refs for i in range(ref.shape[0])]
    key_rows = jnp.concatenate([ref[i, 0, :, lanes] for ref, i in pieces], axis=0)
    value_rows = jnp.concatenate([ref[i, 1, :, lanes] for ref, i in pieces], axis=0)
    scores = lax.dot_general(
        query_rows, key_rows, (((1,), (1,)), ((), ())), preferred_element_type=jnp.float32
    )
    scores = scores + bias
    tiles = [slice(i, i + HD) for i in range(0, scores.shape[1], HD)]
    highest = functools.reduce(jnp.maximum, [scores[:, tile] for tile in tiles])
    if state is not None:
        highest = jnp.maximum(highest, state[0])
    new_max = jnp.max(highest, axis=1, keepdims=True)
    weights = jnp.exp2((scores - new_max) * to_exponent)
    weight_sums = functools.reduce(jnp.add, [weights[:, tile] for tile in tiles])
    mixed = jnp.dot(weights.astype(jnp.bfloat16), value_rows, preferred_element_type=jnp.float32)
    if state is not None:
        shrink = jnp.exp2((state[0] - new_max) * to_exponent)
        weight_sums = weight_sums + state[1] * shrink
        mixed = mixed + state[2] * shrink
    return new_max, weight_sums, mixed


def on_upper():
    return lax.axis_index("span") >= lax.axis_size("span") // 2


def usable_below(clips, offsets):
    chosen = [i for i, (by, _) in enumerate(offsets) if by < clips]
    others = [i for i in range(len(offsets)) if i not in chosen]
    return sorted(chosen + others[: len(chosen) % 2])


def bias_of(bias_ref, first, keys, chosen):
    tiles = [bias_ref[0:1, first + i * keys : first + (i + 1) * keys] for i in chosen]
    return jnp.concatenate(tiles, axis=1)


def put_attended(attended_ref, g, state):
    rows = attended_ref.shape[0]
    mixed = state[2] / jnp.sum(state[1], axis=1, keepdims=True)
    group_size = mixed.shape[0] // rows
    squares = jnp.zeros((rows, HD), jnp.float32)
    for r in range(group_size):
        block = mixed[r * rows : (r + 1) * rows]
        h = g * group_size + r
        attended_ref[:, h * HD : (h + 1) * HD] = block
        squares = squares + block * block
    return squares


def early_kernel(offsets, rows_ref, bias_ref, *refs):
    kv_refs, state_refs, (attended_ref, squares_ref) = refs[:-5], refs[-5:-2], refs[-2:]
    keys = kv_refs[0].shape[2]

    def fold_in(chosen, is_all):
        squares = []
        bias = bias_of(bias_ref, 0, keys, chosen)
        for g in range(rows_ref.shape[0]):
            lanes = slice(g * HD, (g + 1) * HD)
            state = fold(rows_ref[g], [kv_refs[i] for i in chosen], bias, lanes, None)
            if is_all:
                squares.append(put_attended(attended_ref, g, state))
            else:
                state_refs[0][g] = jnp.broadcast_to(state[0], state_refs[0].shape[1:])
                state_refs[1][g] = state[1]
                state_refs[2][g] = state[2]
        if is_all:
            squares_ref[...] = jnp.sum(sum(squares).T, axis=0, keepdims=True)

    pl.when(on_upper())(lambda: fold_in(range(len(kv_refs)), False))
    across = lax.axis_size("span") // 2
    own_clip = lax.axis_index("span")
    middle = jnp.logical_and(own_clip >= 1, own_clip < across)
    pl.when(middle)(lambda: fold_in(usable_below(across, offsets), True))
    pl.when(own_clip == 0)(lambda: fold_in(usable_below(1, offsets), True))


def late_kernel(rows_ref, bias_ref, *refs):
    states, kv_refs, (attended_ref, squares_ref) = refs[:3], refs[5:-2], refs[-2:]
    keys = kv_refs[0].shape[2]
    first = bias_ref.shape[1] - keys * len(kv_refs)

    def end():
        squares = []
        bias = bias_of(bias_ref, first, keys, range(len(kv_refs)))
        for g in range(rows_ref.shape[0]):
            lanes = slice(g * HD, (g + 1) * HD)
            state = fold(rows_ref[g], kv_refs, bias, lanes, [ref[g] for ref in states])
            squares.append(put_attended(attended_ref, g, state))
        squares_ref[...] = jnp.sum(sum(squares).T, axis=0, keepdims=True)

    pl.when(on_upper())(end)


def gain_kernel(attended_ref, factor_ref, live_ref, out_ref):
    live = live_ref[...] > 0.0
    for h in range(attended_ref.shape[1] // HD):
        lanes = slice(h * HD, (h + 1) * HD)
        out_ref[:, lanes] = jnp.where(live, attended_ref[:, lanes] * factor_ref[0:1, lanes], 0.0)


def finish_kernel(features, gained_ref, own_ref, other_ref, out_ref):
    rows = gained_ref.shape[0]
    mean_square = (own_ref[...] + other_ref[...]) / features
    scale = jnp.broadcast_to(lax.rsqrt(mean_square + 1e-06), (HD, rows)).T
    for h in range(gained_ref.shape[1] // HD):
        lanes = slice(h * HD, (h + 1) * HD)
        out_ref[0, :, lanes] = (gained_ref[:, lanes] * scale).astype(out_ref.dtype)


def kernel(body, outs, count, megabytes, name, in_place={}):
    several = isinstance(outs, tuple)
    return pl.pallas_call(
        body,
        out_shape=outs,
        in_specs=in_vmem(count),
        out_specs=tuple(in_vmem(len(outs))) if several else in_vmem(1)[0],
        input_output_aliases=in_place,
        compiler_params=pltpu.CompilerParams(vmem_limit_bytes=megabytes * 1024 * 1024),
        name=name,
    )


def after(array, *others):
    return lax.optimization_barrier((array, *others))[0]


def offsets_of(steps):
    at = {"own": [(0, 0)], "kept": [(0, 0)]}
    for name, hop, source, _ in steps:
        at[name] = [(clip ^ hop[0], part ^ hop[1]) for clip, part in at[source]]
    return at


def travel(steps, own, kept, prepared):
    have = {"own": own, "kept": kept, PREPARED: prepared}
    for name, hop, source, wait_for in steps:
        shard = have[source]
        if wait_for is not None:
            shard = after(shard, have[wait_for])
        have[name] = exchanged(shard, ("span", "seq"), hop)
    return have


def by_exchange(queries, keys_values, clip_tokens, noise_level, level_gate, out_gain):
    tokens_here, width = queries.shape[1:]
    kv_heads_here = keys_values.shape[-1] // HD
    group_size = width // HD // kv_heads_here
    own = keys_values[None, :, 0]
    f32 = functools.partial(jax.ShapeDtypeStruct, dtype=jnp.float32)
    stacked = (kv_heads_here, group_size * tokens_here, HD)
    steps, early, late = plan_of()
    offsets = offsets_of(steps)
    early_at = [at for name in early for at in offsets[name]]
    late_at = [at for name in late for at in offsets[name]]
    offsets = early_at + late_at
    outs = (
        jax.ShapeDtypeStruct(stacked, queries.dtype),
        jax.ShapeDtypeStruct(own.shape, own.dtype),
        f32((8, width)),
        f32((8, tokens_here * len(offsets))),
        f32((tokens_here, HD)),
    )
    sources = (queries[0], level_gate, out_gain, clip_tokens, noise_level, own)
    spaces = (pltpu.VMEM, pltpu.VMEM, pltpu.VMEM, pltpu.SMEM, pltpu.SMEM)
    rows, own_kept, factor, bias, live = pl.pallas_call(
        functools.partial(prepare_kernel, offsets, len(outs)),
        out_shape=outs,
        in_specs=[pl.BlockSpec(memory_space=pltpu.HBM)] * len(sources),
        out_specs=tuple(in_vmem(len(outs))),
        scratch_shapes=[space(x.shape, x.dtype) for space, x in zip(spaces, sources)]
        + [pltpu.SemaphoreType.DMA((len(sources),))],
        compiler_params=pltpu.CompilerParams(vmem_limit_bytes=8 * 1024 * 1024),
        name="prepare",
    )(*(in_hbm(x) for x in sources))
    have = travel(steps, own, own_kept, rows)
    ends = (f32((tokens_here, width)), f32((1, tokens_here)))
    *state, attended, squares = kernel(
        functools.partial(early_kernel, early_at),
        (f32(stacked),) * 3 + ends,
        2 + len(early), 16, "attend_early",
    )(rows, bias, *[have[name] for name in early])
    assert not usable_below(lax.axis_size("span") // 2, late_at)
    attended, squares = kernel(
        late_kernel, ends, 7 + len(late), 16, "attend_late", in_place={5: 0, 6: 1}
    )(rows, bias, *state, attended, squares, *[have[name] for name in late])
    others = [exchanged(squares, ("mp",), (by,)) for by in range(1, lax.axis_size("mp"))]
    gained = kernel(gain_kernel, ends[0], 3, 4, "gain")(attended, factor, live)
    return kernel(
        functools.partial(finish_kernel, width * lax.axis_size("mp")),
        jax.ShapeDtypeStruct(queries.shape, queries.dtype),
        3, 4, "finish",
    )(gained, squares, sum(others))


def passed_along(shard, axis, by):
    peers = lax.axis_size(axis)
    pairs = [(i, i + by) for i in range(peers) if 0 <= i + by < peers]
    return lax.ppermute(shard, axis, pairs)


def by_blocks(queries, keys_values, clip_tokens, noise_level, level_gate, out_gain):
    tokens_here = queries.shape[1]
    slot_count = tokens_here * lax.axis_size("seq")
    clip_count = clip_tokens.shape[0]
    kv_heads_here = keys_values.shape[-1] // HD
    heads_here = queries.shape[-1] // HD
    group_size = heads_here // kv_heads_here
    own_clip = lax.axis_index("span")
    own_seq = lax.axis_index("seq")
    query_heads = queries[0].reshape(tokens_here, kv_heads_here, group_size, HD)
    score_scale = 1.0 / math.sqrt(HD)
    clip_ids = jnp.arange(clip_count, dtype=jnp.int32)

    def clip_length(which):
        return jnp.sum(
            jnp.where(which[:, None] == clip_ids[None, :], clip_tokens[None, :], 0), axis=1
        )

    def block_step(running, key_block, first):
        key_count = key_block.shape[1]
        positions = first + jnp.arange(key_count, dtype=jnp.int32)
        holder = positions // slot_count
        slot_index = positions - holder * slot_count
        usable = (holder >= 0) & (holder <= own_clip) & (slot_index < clip_length(holder))

        def update(state):
            running_max, weight_sum, weighted = state
            key_rows = key_block[0].reshape(key_count, kv_heads_here, HD)
            value_rows = key_block[1].reshape(key_count, kv_heads_here, HD)
            scores = (
                jnp.einsum(
                    "tgrd,kgd->tgrk", query_heads, key_rows, preferred_element_type=jnp.float32
                )
                * score_scale
            )
            scores = jnp.where(usable[None, None, None, :], scores, -jnp.inf)
            new_max = jnp.maximum(running_max, jnp.max(scores, axis=-1))
            weights = jnp.exp(scores - new_max[..., None])
            shrink = jnp.exp(running_max - new_max)
            weight_sum = weight_sum * shrink + jnp.sum(weights, axis=-1)
            weighted = weighted * shrink[..., None] + jnp.einsum(
                "tgrk,kgd->tgrd",
                weights.astype(jnp.bfloat16),
                value_rows,
                preferred_element_type=jnp.float32,
            )
            return (new_max, weight_sum, weighted)

        def unchanged(state):
            return state

        return lax.cond(jnp.any(usable), update, unchanged, running)

    def fold_piece(running, kv_piece, first):
        key_count = kv_piece.shape[1]
        if key_count > 1024 and key_count % 1024 == 0:

            def loop_step(block_index, state):
                key_block = lax.dynamic_slice_in_dim(kv_piece, block_index * 1024, 1024, 1)
                return block_step(state, key_block, first + block_index * 1024)

            return lax.fori_loop(0, key_count // 1024, loop_step, running)
        return block_step(running, kv_piece, first)

    initial = (
        jnp.full((tokens_here, kv_heads_here, group_size), -jnp.inf, jnp.float32),
        jnp.zeros((tokens_here, kv_heads_here, group_size), jnp.float32),
        jnp.zeros((tokens_here, kv_heads_here, group_size, HD), jnp.float32),
    )
    local_kv = keys_values[:, 0]
    clip_kv = lax.all_gather(local_kv, "seq", axis=1, tiled=True)
    running = fold_piece(initial, clip_kv, own_clip * slot_count)
    for distance in range(1, clip_count):
        clip_kv = passed_along(clip_kv, "span", 1)
        running = fold_piece(running, clip_kv, (own_clip - distance) * slot_count)
    running_max, weight_sum, weighted = running
    attended = (weighted / weight_sum[..., None]).reshape(
        tokens_here, kv_heads_here * group_size * HD
    )
    squares = jnp.sum(attended * attended, axis=1)
    mean_square = lax.psum(squares, "mp") / (heads_here * HD * lax.axis_size("mp"))
    own_level = jnp.sum(jnp.where(clip_ids == own_clip, noise_level, 0))
    one_hot = (jnp.arange(level_gate.shape[0], dtype=jnp.int32) == own_level).astype(jnp.bfloat16)
    gate_row = jnp.dot(one_hot, level_gate, preferred_element_type=jnp.float32)
    own_length = jnp.sum(jnp.where(clip_ids == own_clip, clip_tokens, 0))
    usable_rows = own_seq * tokens_here + jnp.arange(tokens_here, dtype=jnp.int32) < own_length
    normed = (
        attended
        * lax.rsqrt(mean_square + 1e-06)[:, None]
        * out_gain.astype(jnp.float32)
        * (1.0 + gate_row)
    )
    return jnp.where(usable_rows[:, None], normed, 0.0).astype(jnp.bfloat16)[None]


def per_device(*arrays):
    sizes = tuple(lax.axis_size(axis) for axis in ("span", "seq", "mp"))
    few = sizes == (4, 4, 2)
    return (by_exchange if few else by_blocks)(*arrays)


def solution(mesh):
    placed = (
        P("span", "seq", "mp"),
        P(None, "span", "seq", "mp"),
        P(),
        P(),
        P(None, "mp"),
        P("mp"),
    )
    return jax.shard_map(
        per_device, mesh=mesh, in_specs=placed, out_specs=P("span", "seq", "mp"), check_vma=False
    )
```
